512 devices in a mesh: grp: 64 (over x, z), dev: 8 (over y, core).
Axes of the slice: x: 4, y: 4, z: 16, core: 2. Of those that a mesh axis runs over, the one named last changes fastest.
Arguments:
- tokens: bfloat16 [32768, 768], P(('grp', 'dev')), may hold values from -6 to 6
- expert_ids: int32 [32768, 8], P(('grp', 'dev')), may hold values from 0 to 511, as said below
- gates: bfloat16 [32768, 8], P(('grp', 'dev')), may hold values from 0.099609375 to 0.5
- w_in: bfloat16 [512, 768, 1536], P(('grp', 'dev')), may hold values from -0.21875 to 0.21875
- w_out: bfloat16 [512, 1536, 768], P(('grp', 'dev')), may hold values from -0.15625 to 0.15625
Outputs:
- mixed: bfloat16 [32768, 768], P(('grp', 'dev'))
The draws below stay inside these ranges and needn't reach their ends.
Inputs may be any that keep to these rules, and one draw needn't show every extreme that they name: `expert_ids`: row t lists 8 experts; columns 2 * k and 2 * k + 1 are two different experts of one group (experts g * 8 to g * 8 + 7 form group g), and the four groups of a row differ. The owner of token t is t // 64, and its dev index is the owner modulo 8. The tokens of one owner pick one group at most 12 times, and every owner reaches it for some group. The tokens whose owners share a dev index pick each group exactly 4 * 64 times in all and each expert at most 192 times; in every group one expert is picked 192 times by the tokens of every dev index.
All inputs are finite; a program needn't handle non-finite values.
Results may differ from the reference program's by a relative error of at most 0.0057.
Values may be sent and summed in bfloat16 or wider, within the bound.
A program may use at most 64 MiB of HBM per device.

```python
import jax
import jax.numpy as jnp
from jax import lax

D = 768
FF = 1536
PICKS = 8
TOK_DEV = 64
EXPERTS = 512
TOKENS = 32768
CAP_G = 12
CAP_E = 192
N_GRP = 64
N_DEV = 8


def draw_expert_ids(key, part):
    slots = 4 * TOK_DEV
    base = jax.random.fold_in(key, 11)
    key_shift, key_group, key_hot, key_rest = jax.random.split(base, 4)
    shift_perm = jax.vmap(lambda sub: jax.random.permutation(sub, N_GRP))(jax.random.split(key_shift, N_DEV))
    group_perm = jax.random.permutation(key_group, N_GRP)
    group_inverse = jnp.argsort(group_perm)
    hot_expert = jax.random.randint(key_hot, (N_GRP,), 0, N_DEV)
    rest_perm = jax.vmap(lambda sub: jax.random.permutation(sub, N_DEV - 1))(jax.random.split(key_rest, N_GRP * N_DEV))
    rest_perm = rest_perm.reshape(N_GRP, N_DEV, N_DEV - 1) + 1
    rotation = jnp.concatenate([jnp.zeros((N_GRP, N_DEV, 1), jnp.int32), rest_perm.astype(jnp.int32)], axis=2)
    run_index = (group_inverse[None, :, None] - shift_perm[:, None, :]) % N_GRP
    run_length = jnp.clip(slots - run_index * CAP_G, 0, CAP_G)
    prefix = jnp.cumsum(run_length, axis=2) - run_length
    source_grp = jnp.arange(N_GRP)[:, None, None]
    source_dev = jnp.arange(N_DEV)[None, :, None]
    slot_index = jnp.arange(slots)[None, None, :]
    slot_run = slot_index // CAP_G
    rotated = (slot_run + shift_perm[source_dev, source_grp]) % N_GRP
    relay_group = group_perm[rotated]
    relay_row = prefix[source_dev, relay_group, source_grp] + slot_index % CAP_G
    bounds = CAP_E + (jnp.arange(1, N_DEV) - 1) * (2 * slots - CAP_E) // (N_DEV - 1)

    def expert_of(position):
        run_number = jnp.sum((position[..., None] >= bounds).astype(jnp.int32), axis=-1)
        return (hot_expert[relay_group] + rotation[relay_group, source_dev, run_number]) % N_DEV
    first_pick = relay_group * N_DEV + expert_of(relay_row)
    second_pick = relay_group * N_DEV + expert_of(relay_row + slots)
    stacked = jnp.stack([first_pick, second_pick], axis=-1)
    stacked = stacked.reshape(N_GRP, N_DEV, 4, TOK_DEV, 2).transpose(0, 1, 3, 2, 4)
    return stacked.reshape(N_GRP * N_DEV * TOK_DEV, 8).astype(jnp.int32)


def level_of(stream_key, extent, shards, least, high):
    def one(dim, parts):
        steps = jax.random.uniform(jax.random.fold_in(jax.random.fold_in(stream_key, 6), dim), (parts,), jnp.float32, least / len(shards), high / len(shards))
        return jnp.repeat(jnp.exp(steps), extent[dim] // parts).reshape((-1,) + (1,) * (len(extent) - dim - 1))

    loudness = one(*shards[0])
    for cut in shards[1:]:
        loudness = loudness * one(*cut)
    return loudness


def normal_values(key, shape, deviation, bound, pieces=(), held_as=jnp.bfloat16):
    entries = jax.random.normal(key, shape, jnp.float32) * deviation
    if len(pieces) > 0:
        entries = level_of(key, shape, pieces, -0.22, 0.18) * entries
    return jnp.clip(entries, min=-bound, max=bound).astype(held_as)


def setup_inputs(seed: int = 0) -> dict:
    seeds = jax.random.split(jax.random.key(seed), 6)
    return {
        "tokens": normal_values(seeds[0], (TOKENS, D), 1.0, 6.0, ((0, 512),)),
        "expert_ids": draw_expert_ids(jax.random.fold_in(seeds[5], 71), 0),
        "gates": jnp.clip(0.099609375 + 0.40039062 * jax.random.uniform(seeds[2], (TOKENS, PICKS), jnp.float32) ** level_of(seeds[2], (TOKENS, PICKS), ((0, 512),), -0.2, 0.2), 0.099609375, 0.5).astype(jnp.bfloat16),
        "w_in": normal_values(seeds[3], (EXPERTS, D, FF), D ** -0.5, 0.21875, ((0, 512),)),
        "w_out": normal_values(seeds[4], (EXPERTS, FF, D), FF ** -0.5, 0.15625, ((0, 512),)),
    }


def reference(tokens, expert_ids, gates, w_in, w_out):
    flat_ids = expert_ids.reshape(-1)
    flat_gates = gates.reshape(-1).astype(jnp.float32)
    pair_total = flat_ids.shape[0]
    capacity = N_DEV * CAP_E

    def expert_step(running, expert):
        picked = jnp.nonzero(flat_ids == expert, size=capacity, fill_value=pair_total)[0].astype(jnp.int32)
        in_range = picked < pair_total
        token_rows = jnp.minimum(picked // PICKS, TOKENS - 1).astype(jnp.int32)
        gathered = jnp.take(tokens, token_rows, axis=0).astype(jnp.float32)
        hidden = jnp.maximum(jnp.dot(gathered, w_in[expert].astype(jnp.float32), preferred_element_type=jnp.float32), 0.0).astype(jnp.bfloat16)
        output = jnp.dot(hidden.astype(jnp.float32), w_out[expert].astype(jnp.float32), preferred_element_type=jnp.float32).astype(jnp.bfloat16)
        weights_row = jnp.where(in_range, jnp.take(flat_gates, jnp.minimum(picked, pair_total - 1).astype(jnp.int32)), 0.0)
        running = running.at[token_rows].add(weights_row[:, None] * output.astype(jnp.float32))
        return running, None

    start = jnp.zeros((TOKENS, D), jnp.float32)
    running, unused = lax.scan(expert_step, start, jnp.arange(EXPERTS, dtype=jnp.int32))
    return running.astype(jnp.bfloat16)
```

```python
import jax
import jax.numpy as jnp
from jax import lax
from jax.sharding import PartitionSpec as P

F32 = jnp.float32
BF16 = jnp.bfloat16
NX = 4
NZ = 16


def per_device(tokens, expert_ids, gates, w_in, w_out):
    n_dev = lax.axis_size("dev")
    count, width = tokens.shape
    cap = 4 * count
    z_sets = [[x * NZ + z for z in range(NZ)] for x in range(NX)]
    x_sets = [[x * NZ + z for x in range(NX)] for z in range(NZ)]
    me = lax.axis_index("grp")
    my_x, my_z = me // NZ, me % NZ
    mine = lax.axis_index("dev")

    pairs = expert_ids.reshape(count, 4, 2)
    gate_pairs = gates.reshape(count, 4, 2)
    meta = jnp.concatenate(
        [
            (pairs[:, :, 0] // n_dev).astype(BF16),
            (pairs[:, :, 0] % n_dev).astype(BF16),
            (pairs[:, :, 1] % n_dev).astype(BF16),
            gate_pairs[:, :, 0],
            gate_pairs[:, :, 1],
        ],
        axis=1,
    ).T
    column = lax.all_gather(tokens, "grp", axis_index_groups=z_sets, tiled=True)
    metas = lax.all_gather(meta, "grp")
    group = metas[:, 0:4, :].astype(jnp.int32)
    tri = (jnp.arange(count)[:, None] < jnp.arange(count)[None, :]).astype(BF16)
    owners = NX * NZ
    tri_o = (jnp.arange(owners)[:, None] < jnp.arange(owners)[None, :]).astype(F32)
    targets = jnp.arange(NX) * NZ + my_z
    match = (group[None] == targets[:, None, None, None]).astype(BF16)
    hit = jnp.sum(match, axis=2)
    within = jnp.dot(hit, tri, preferred_element_type=F32)
    totals = jnp.sum(hit.astype(F32), axis=2)
    base = jnp.dot(totals, tri_o, precision=lax.Precision.HIGHEST)
    place = jnp.where(hit > 0, within + base[:, :, None], -1.0).astype(jnp.int32)
    own = lax.dynamic_slice_in_dim(place, my_x * NZ, NZ, axis=1).reshape(NX, NZ * count)
    rows = jnp.arange(cap)
    select = (own[:, None, :] == rows[None, :, None]).astype(BF16).reshape(NX * cap, NZ * count)
    spread = jnp.dot(select, column, preferred_element_type=F32).astype(BF16)
    group_rows = lax.psum_scatter(
        spread, "grp", scatter_dimension=0, axis_index_groups=x_sets, tiled=True
    )
    all_rows = lax.all_gather(group_rows, "dev", tiled=True)

    place_me = lax.dynamic_index_in_dim(place, my_x, 0, keepdims=False).reshape(-1)
    match_me = lax.dynamic_index_in_dim(match, my_x, 0, keepdims=False)
    facts = jnp.stack(
        [jnp.sum(match_me * metas[:, 4 * i : 4 * i + 4, :], axis=1) for i in range(1, 5)], axis=-1
    ).reshape(owners * count, 4)
    seat = (place_me[None, :] == rows[:, None]).astype(BF16)
    row_facts = jnp.dot(seat, facts, preferred_element_type=F32).astype(BF16)
    all_facts = lax.all_gather(row_facts, "dev", tiled=True)
    who = mine.astype(BF16)
    weight = jnp.where(all_facts[:, 0] == who, all_facts[:, 2], 0).astype(F32) + jnp.where(
        all_facts[:, 1] == who, all_facts[:, 3], 0
    ).astype(F32)

    hidden = jnp.maximum(jnp.dot(all_rows, w_in[0], preferred_element_type=F32), 0.0).astype(BF16)
    out = jnp.dot(hidden, w_out[0], preferred_element_type=F32)
    out = (out * weight[:, None]).astype(BF16)
    group_sum = lax.psum_scatter(out, "dev", scatter_dimension=0, tiled=True)
    back = lax.all_gather(group_sum, "grp", axis_index_groups=x_sets, tiled=True)
    partial_sum = lax.dot_general(
        select, back, (((0,), (0,)), ((), ())), preferred_element_type=F32
    ).astype(BF16)
    return lax.psum_scatter(
        partial_sum, "grp", scatter_dimension=0, axis_index_groups=z_sets, tiled=True
    )


def solution(mesh):
    tok = P(("grp", "dev"), None)
    return jax.shard_map(
        per_device,
        mesh=mesh,
        in_specs=(tok, tok, tok, P(("grp", "dev"), None, None), P(("grp", "dev"), None, None)),
        out_specs=tok,
        check_vma=False,
    )
```

```python
import jax
import jax.numpy as jnp
from jax import lax
from jax.experimental import pallas as pl
from jax.experimental.pallas import tpu as pltpu
from jax.sharding import PartitionSpec as P

F32 = jnp.float32
BF16 = jnp.bfloat16
NX = 4
NY = 4
NZ = 16
TOK = 64
D = 768
FF = 1536
HALF = 384
CAP = 256
COPIES = 160
MESH = pl.DeviceIdType.MESH
NT = (((1,), (1,)), ((), ()))


def iota(shape, dim):
    return lax.broadcasted_iota(jnp.int32, shape, dim)


def ones_where(cond):
    return jnp.where(cond, 1.0, 0.0).astype(BF16)


def mm(a, b):
    return jnp.dot(a, b, preferred_element_type=F32)


def kernel(
    tok_ref,
    meta_ref,
    w1_hbm,
    w2_hbm,
    out_ref,
    w1,
    w2,
    column,
    metas,
    meta_x,
    places,
    facts_q,
    select,
    select_t,
    spread,
    mid,
    fin,
    rows,
    row_facts,
    outs,
    peer,
    back,
    partial_sum,
    ring_in,
    ring_out,
    load_sem,
    send_sem,
    recv_sem,
):
    grp, dev = lax.axis_index("grp"), lax.axis_index("dev")
    x, z = grp // NZ, lax.rem(grp, NZ)
    y, c = dev // 2, lax.rem(dev, 2)
    z_next = (x * NZ + lax.rem(z + 1, NZ), dev)
    z_prev = (x * NZ + lax.rem(z + NZ - 1, NZ), dev)
    x_next = (lax.rem(x + 1, NX) * NZ + z, dev)
    x_prev = (lax.rem(x + NX - 1, NX) * NZ + z, dev)
    y_next = (grp, lax.rem(y + 1, NY) * 2 + c)
    y_prev = (grp, lax.rem(y + NY - 1, NY) * 2 + c)
    twin = (grp, y * 2 + 1 - c)

    load1 = pltpu.make_async_copy(w1_hbm.at[0], w1, load_sem.at[0])
    load2 = pltpu.make_async_copy(w2_hbm.at[0], w2, load_sem.at[1])
    load1.start()
    load2.start()

    barrier = pltpu.get_barrier_semaphore()
    for neighbour in (z_next, z_prev, x_next, x_prev, y_next, y_prev, twin):
        pl.semaphore_signal(barrier, inc=1, device_id=neighbour, device_id_type=MESH)
    pl.semaphore_wait(barrier, 7)

    started = []

    def send(src, dst, to):
        k = len(started)
        copy = pltpu.make_async_remote_copy(
            src_ref=src,
            dst_ref=dst,
            send_sem=send_sem.at[k],
            recv_sem=recv_sem.at[k],
            device_id=to,
            device_id_type=MESH,
        )
        copy.start()
        started.append(copy)
        return copy

    def block(r, h):
        return column.at[pl.ds((r % NZ) * TOK + h * 32, 32)]

    def pass_on(step, before):
        made = {}
        for h in range(2):
            for way, to in ((1, z_next), (-1, z_prev)):
                if (h, way) in before:
                    before[h, way].wait_recv()
                if step == 8 and h != (way < 0):
                    continue
                held = -way * (step - 1)
                src = tok_ref.at[pl.ds(h * 32, 32)] if step == 1 else block(held, h)
                made[h, way] = send(src, block(held - way, h), to)
        return made

    tokens_in = pass_on(1, {})
    m_up = send(meta_ref, meta_x.at[0], x_next)
    m_down = send(meta_ref, meta_x.at[1], x_prev)
    column[0:TOK, :] = tok_ref[...]
    m_up.wait_recv()
    m_far = send(meta_x.at[0], meta_x.at[2], x_next)
    m_down.wait_recv()
    m_far.wait_recv()
    metas[0:16, :] = meta_ref[...] + meta_x[0] + meta_x[1] + meta_x[2]

    def bundle(r):
        return metas.at[pl.ds((r % NZ) * 16, 16)]

    def pass_meta(step):
        made = [send(bundle(-(step - 1)), bundle(-step), z_next)]
        if step < 8:
            made.append(send(bundle(step - 1), bundle(step), z_prev))
        return made

    metas_in = pass_meta(1)
    for step in range(2, 9):
        tokens_in = pass_on(step, tokens_in)
        for copy in metas_in:
            copy.wait_recv()
        metas_in = pass_meta(step)
    for copy in metas_in:
        copy.wait_recv()

    group_of = metas[:, 0:128].astype(F32)
    match = []
    for i in range(NX):
        target = lax.rem(x + i, NX) * NZ + z
        match.append(jnp.where(group_of == target.astype(F32), 1.0, 0.0))
    sum_k = ones_where(lax.shift_right_logical(iota((64, 256), 1), 2) == iota((64, 256), 0))
    hits = jnp.concatenate([mm(sum_k, m.astype(BF16)) for m in match], axis=0)
    hits_b = hits.astype(BF16)
    lane_r, lane_c = iota((128, 128), 0), iota((128, 128), 1)
    before = ones_where((lane_r < lane_c) & ((lane_r < 64) == (lane_c < 64)))
    counts = mm(hits_b, ones_where(lane_r < 64))
    own_r, own_c = iota((256, 256), 0), iota((256, 256), 1)
    earlier = ones_where(
        (own_c < own_r) & (lax.shift_right_logical(own_c, 6) == lax.shift_right_logical(own_r, 6))
    )
    place = jnp.where(hits > 0, mm(hits_b, before) + mm(earlier, counts.astype(BF16)), -1.0)
    place_b = place.astype(BF16)
    fold_r, fold_c = iota((32, 256), 0), iota((32, 256), 1)
    first = (
        lax.shift_right_logical(fold_r, 3) * 64 + jnp.bitwise_and(fold_r, 7) * 8 + x
    )
    low = iota((32, 128), 1) < 64
    own_places = jnp.where(
        low,
        mm(ones_where(fold_c == first), place_b),
        mm(ones_where(fold_c == first + 4), place_b),
    )
    places[0:32, :] = own_places

    row_id = iota((CAP, 128), 0).astype(F32)

    def build_select(i):
        for b in range(8):
            select[pl.ds(i * CAP, CAP), b * 128 : (b + 1) * 128] = ones_where(
                row_id == places[i * 8 + b : i * 8 + b + 1, :]
            )

    def spread_one(i):
        build_select(i)
        got = mm(select[pl.ds(i * CAP, CAP), :], column[...]).astype(BF16)
        spread[i, 0] = got[:, 0:HALF]
        spread[i, 1] = got[:, HALF:D]

    def top(r):
        return pl.ds(r * 128, 128)

    for i in (2,):
        build_select(i)
    for copy in tokens_in.values():
        copy.wait_recv()

    def reduce_first(buf, nxt, prv):
        return (
            [send(buf.at[2, 0, top(r)], mid.at[nxt[1], 0, top(r)], prv[0]) for r in range(2)],
            [send(buf.at[2, 1, top(r)], mid.at[nxt[1], 1, top(r)], nxt[0]) for r in range(2)],
        )

    def reduce_direct(buf, i, nxt, prv):
        if i == 3:
            return [send(buf.at[3, 1, top(r)], fin.at[nxt[1], 0, 1, top(r)], prv[0]) for r in range(2)]
        return [send(buf.at[1, 0, top(r)], fin.at[nxt[1], 1, 0, top(r)], nxt[0]) for r in range(2)]

    def reduce_merge(buf, firsts, nxt, prv):
        made = []
        for r in range(2):
            rr = slice(r * 128, (r + 1) * 128)
            firsts[0][r].wait_recv()
            buf[3, 0, rr, :] = (
                buf[3, 0, rr, :].astype(F32) + mid[nxt[1], 0, rr, :].astype(F32)
            ).astype(BF16)
            made.append(send(buf.at[3, 0, top(r)], fin.at[nxt[1], 0, 0, top(r)], prv[0]))
            firsts[1][r].wait_recv()
            buf[1, 1, rr, :] = (
                buf[1, 1, rr, :].astype(F32) + mid[nxt[1], 1, rr, :].astype(F32)
            ).astype(BF16)
            made.append(send(buf.at[1, 1, top(r)], fin.at[nxt[1], 1, 1, top(r)], nxt[0]))
        return made

    def reduce_sum(buf, which, h):
        return (
            buf[0, h].astype(F32) + fin[which, 0, h].astype(F32) + fin[which, 1, h].astype(F32)
        ).astype(BF16)

    xn, xp = (x_next, 0), (x_prev, 0)
    got = mm(select[pl.ds(2 * CAP, CAP), :], column[...]).astype(BF16)
    spread[2, 0] = got[:, 0:HALF]
    spread[2, 1] = got[:, HALF:D]
    firsts = reduce_first(spread, xn, xp)
    spread_one(3)
    finals = reduce_direct(spread, 3, xn, xp)
    spread_one(1)
    finals += reduce_direct(spread, 1, xn, xp)
    finals += reduce_merge(spread, firsts, xn, xp)
    spread_one(0)

    match_own = match[0].astype(BF16)
    fact_a = mm(sum_k, match_own * metas[:, 128:256]).astype(BF16)
    fact_b = mm(sum_k, match_own * metas[:, 256:384]).astype(BF16)
    swap = ones_where((lane_r + 64 == lane_c) | (lane_r == lane_c + 64))
    four = jnp.concatenate(
        [fact_a, mm(fact_a, swap).astype(BF16), fact_b, mm(fact_b, swap).astype(BF16)], axis=1
    )
    pick_r, pick_c = iota((32, 64), 0), iota((32, 64), 1)
    even, odd = ones_where(pick_c == 2 * pick_r), ones_where(pick_c == 2 * pick_r + 1)
    four_e, four_o = mm(even, four), mm(odd, four)
    place_own = place_b[0:64, :]
    places[32:64, :] = jnp.where(low, mm(even, place_own), mm(odd, place_own))
    stack = jnp.concatenate(
        [
            jnp.where(low, four_e[:, 0:128], four_o[:, 128:256]),
            jnp.where(low, four_e[:, 128:256], four_o[:, 0:128]),
            jnp.where(low, four_e[:, 256:384], four_o[:, 384:512]),
            jnp.where(low, four_e[:, 384:512], four_o[:, 256:384]),
        ],
        axis=0,
    ).astype(BF16)
    q_r, q_c = iota((256, 128), 0), iota((256, 128), 1)
    deal = ones_where(
        (jnp.bitwise_and(q_r, 7) == lax.shift_right_logical(q_c, 5))
        & (lax.shift_right_logical(q_r, 3) == jnp.bitwise_and(q_c, 31))
    )
    facts_q[...] = mm(deal, stack)

    def gather_facts(b, total):
        hot = ones_where(row_id == places[pl.ds(32 + b, 1), :])
        return total + lax.dot_general(
            facts_q[pl.ds(pl.multiple_of(b * 8, 8), 8), :].astype(BF16),
            hot,
            NT,
            preferred_element_type=F32,
        )

    row_facts[0, 0] = lax.fori_loop(0, 32, gather_facts, jnp.zeros((8, CAP), F32))

    eye = ones_where(lane_r == lane_c)
    places_t = lax.dot_general(eye, own_places.astype(BF16), NT, preferred_element_type=F32)
    lane_id = iota((128, CAP), 1).astype(F32)
    for i in range(NX):
        for b in range(8):
            k = i * 8 + b
            select_t[b * 128 : (b + 1) * 128, i * CAP : (i + 1) * CAP] = ones_where(
                lane_id == places_t[:, k : k + 1]
            )

    for copy in finals:
        copy.wait_recv()
    rows[0, 0, :, 0:HALF] = reduce_sum(spread, 0, 0)
    rows[0, 0, :, HALF:D] = reduce_sum(spread, 0, 1)

    up, down = [], []
    for r in range(2):
        up.append(send(rows.at[0, 0, top(r)], rows.at[3, 0, top(r)], y_next))
        down.append(send(rows.at[0, 0, top(1 - r)], rows.at[1, 0, top(1 - r)], y_prev))
    across = [send(rows.at[0, 0], rows.at[0, 1], twin), send(row_facts.at[0, 0], row_facts.at[0, 1], twin)]
    f_up = send(row_facts.at[0, 0], row_facts.at[3, 0], y_next)
    f_down = send(row_facts.at[0, 0], row_facts.at[1, 0], y_prev)

    eye_rows = ones_where(own_r == own_c)
    expert = dev.astype(F32)

    def feed_forward(i):
        block_in = rows[i].reshape(2 * CAP, D)

        def part(n, total):
            lo = pl.multiple_of(n * 512, 512)
            hidden = jnp.maximum(mm(block_in, w1[:, pl.ds(lo, 512)]), 0.0).astype(BF16)
            return total + mm(hidden, w2[pl.ds(lo, 512), :])

        total = lax.fori_loop(0, FF // 512, part, jnp.zeros((2 * CAP, D), F32))
        for core in range(2):
            f = row_facts[i, core]
            weight = jnp.where(f[0:1] == expert, f[2:3], 0.0) + jnp.where(f[1:2] == expert, f[3:4], 0.0)
            weight = jnp.broadcast_to(weight, (128, CAP)).astype(BF16)
            weight = lax.dot_general(eye_rows, weight, NT, preferred_element_type=F32)
            for n in range(6):
                outs[core, i, n // 3, :, (n % 3) * 128 : (n % 3 + 1) * 128] = (
                    total[core * CAP : (core + 1) * CAP, n * 128 : (n + 1) * 128] * weight
                ).astype(BF16)
        return send(outs.at[1, i], peer.at[i], twin)

    def join_cores(i, copy):
        copy.wait_recv()
        for h in range(2):
            outs[0, i, h] = (outs[0, i, h].astype(F32) + peer[i, h].astype(F32)).astype(BF16)

    load1.wait()
    load2.wait()
    for copy in across:
        copy.wait_recv()
    joins = {0: feed_forward(0)}
    far = []
    up[0].wait_recv()
    far.append(send(rows.at[3, 0, top(0)], rows.at[2, 0, top(0)], y_next))
    down[0].wait_recv()
    far.append(send(rows.at[1, 0, top(1)], rows.at[2, 0, top(1)], y_prev))
    f_up.wait_recv()
    far.append(send(row_facts.at[3, 0], row_facts.at[2, 0], y_next))
    up[1].wait_recv()
    across = {3: [send(rows.at[3, 0], rows.at[3, 1], twin), send(row_facts.at[3, 0], row_facts.at[3, 1], twin)]}
    down[1].wait_recv()
    f_down.wait_recv()
    across[1] = [send(rows.at[1, 0], rows.at[1, 1], twin), send(row_facts.at[1, 0], row_facts.at[1, 1], twin)]
    yn, yp = (y_next, 1), (y_prev, 1)
    out_own = outs.at[0]
    for copy in across[3]:
        copy.wait_recv()
    joins[3] = feed_forward(3)
    for copy in far:
        copy.wait_recv()
    across[2] = [send(rows.at[2, 0], rows.at[2, 1], twin), send(row_facts.at[2, 0], row_facts.at[2, 1], twin)]
    join_cores(3, joins[3])
    finals = reduce_direct(out_own, 3, yn, yp)
    for copy in across[1]:
        copy.wait_recv()
    joins[1] = feed_forward(1)
    for copy in across[2]:
        copy.wait_recv()
    join_cores(1, joins[1])
    finals += reduce_direct(out_own, 1, yn, yp)
    joins[2] = feed_forward(2)
    join_cores(2, joins[2])
    firsts = reduce_first(out_own, yn, yp)
    join_cores(0, joins[0])
    finals += reduce_merge(out_own, firsts, yn, yp)
    for copy in finals:
        copy.wait_recv()
    for h in range(2):
        back[0:CAP, h * HALF : (h + 1) * HALF] = reduce_sum(out_own, 1, h)

    def back_half(i, r):
        return back.at[pl.ds(i * CAP + r * 128, 128)]

    up, down, far = [], [], []
    for r in range(2):
        up.append(send(back_half(0, r), back_half(3, r), x_next))
        down.append(send(back_half(0, 1 - r), back_half(1, 1 - r), x_prev))
    up[0].wait_recv()
    far.append(send(back_half(3, 0), back_half(2, 0), x_next))
    down[0].wait_recv()
    far.append(send(back_half(1, 1), back_half(2, 1), x_prev))
    for copy in (up[1], down[1], *far):
        copy.wait_recv()

    def to_tokens(m, carry):
        at = pl.ds(pl.multiple_of(m * 256, 256), 256)
        partial_sum[at, :] = mm(select_t[at, :], back[...])
        return carry

    lax.fori_loop(0, 4, to_tokens, 0)

    arrived = {}
    for step in range(1, 9):
        current = {}
        for h in range(2):
            for w, way, to in ((0, -1, z_prev), (1, 1, z_next)):
                if step == 1 and h != w:
                    continue
                target = (way * (9 - step)) % NZ
                at = slice(target * TOK + h * 32, target * TOK + h * 32 + 32)
                value = partial_sum[at, :]
                if (w, h) in arrived:
                    arrived[w, h].wait_recv()
                    value = value + ring_in[w, step - 2, h * 32 : h * 32 + 32, :].astype(F32)
                ring_out[w, step - 1, h * 32 : h * 32 + 32, :] = value.astype(BF16)
                part = pl.ds(h * 32, 32)
                current[w, h] = send(ring_out.at[w, step - 1, part], ring_in.at[w, step - 1, part], to)
        arrived = current
    for copy in arrived.values():
        copy.wait_recv()
    out_ref[...] = (
        partial_sum[0:TOK, :] + ring_in[0, 7].astype(F32) + ring_in[1, 7].astype(F32)
    ).astype(BF16)

    for copy in started:
        copy.wait_send()


def per_device(tokens, expert_ids, gates, w_in, w_out):
    x = lax.axis_index("grp") // NZ
    pairs = expert_ids.reshape(TOK, 4, 2)
    gate_pairs = gates.reshape(TOK, 4, 2)
    group = (pairs[:, :, 0] // 8).astype(BF16)
    fields = jnp.stack(
        [
            group,
            group,
            (pairs[:, :, 0] % 8).astype(BF16),
            (pairs[:, :, 1] % 8).astype(BF16),
            gate_pairs[:, :, 0],
            gate_pairs[:, :, 1],
        ]
    )
    fields = fields.transpose(2, 0, 1).reshape(4, 6 * TOK)
    meta = jnp.where((jnp.arange(16) // 4 == x)[:, None], jnp.tile(fields, (4, 1)), 0)
    vmem = pl.BlockSpec(memory_space=pltpu.VMEM)
    hbm = pl.BlockSpec(memory_space=pl.ANY)
    return pl.pallas_call(
        kernel,
        out_shape=jax.ShapeDtypeStruct((TOK, D), BF16),
        in_specs=[vmem, vmem, hbm, hbm],
        out_specs=vmem,
        scratch_shapes=[
            pltpu.VMEM((D, FF), BF16),
            pltpu.VMEM((FF, D), BF16),
            pltpu.VMEM((NZ * TOK, D), BF16),
            pltpu.VMEM((NZ * 16, 384), BF16),
            pltpu.VMEM((3, 16, 384), BF16),
            pltpu.VMEM((64, 128), F32),
            pltpu.VMEM((256, 128), F32),
            pltpu.VMEM((NX * CAP, NZ * TOK), BF16),
            pltpu.VMEM((NZ * TOK, NX * CAP), BF16),
            pltpu.VMEM((4, 2, CAP, HALF), BF16),
            pltpu.VMEM((2, 2, CAP, HALF), BF16),
            pltpu.VMEM((2, 2, 2, CAP, HALF), BF16),
            pltpu.VMEM((4, 2, CAP, D), BF16),
            pltpu.VMEM((4, 2, 8, CAP), F32),
            pltpu.VMEM((2, 4, 2, CAP, HALF), BF16),
            pltpu.VMEM((4, 2, CAP, HALF), BF16),
            pltpu.VMEM((NX * CAP, D), BF16),
            pltpu.VMEM((NZ * TOK, D), F32),
            pltpu.VMEM((2, 8, TOK, D), BF16),
            pltpu.VMEM((2, 8, TOK, D), BF16),
            pltpu.SemaphoreType.DMA((2,)),
            pltpu.SemaphoreType.DMA((COPIES,)),
            pltpu.SemaphoreType.DMA((COPIES,)),
        ],
        compiler_params=pltpu.CompilerParams(
            collective_id=0, has_side_effects=True, vmem_limit_bytes=56 * 1024 * 1024
        ),
        cost_estimate=pl.CostEstimate(
            flops=15_000_000_000, bytes_accessed=5_000_000, transcendentals=0
        ),
    )(tokens, meta, w_in, w_out)


def solution(mesh):
    tok = P(("grp", "dev"), None)
    return jax.shard_map(
        per_device,
        mesh=mesh,
        in_specs=(tok, tok, tok, P(("grp", "dev"), None, None), P(("grp", "dev"), None, None)),
        out_specs=tok,
        check_vma=False,
    )
```

```python
import jax
import jax.numpy as jnp
from jax import lax
from jax.experimental import pallas as pl
from jax.experimental.pallas import tpu as pltpu
from jax.sharding import PartitionSpec as P

F32 = jnp.float32
BF16 = jnp.bfloat16
NX = 4
NY = 4
NZ = 16
TOK = 64
D = 768
FF = 1536
HALF = 384
CAP = 256
WIDE = 896
SLOT = 12
QUAD = 48
COPIES = 240
PIECES = 4
PIECE = 16
ORDER = (0, 1, -1, 2, -2, 3, -3, 4, -4, 5, -5, 6, -6, 7, -7, 8)
MESH = pl.DeviceIdType.MESH
NT = (((1,), (1,)), ((), ()))


def iota(shape, dim):
    return lax.broadcasted_iota(jnp.int32, shape, dim)


def ones_where(cond):
    return jnp.where(cond, 1.0, 0.0).astype(BF16)


def mm(a, b):
    return jnp.dot(a, b, preferred_element_type=F32)


def kernel(
    tok_ref,
    w1_hbm,
    w2_hbm,
    out_ref,
    w1,
    w2,
    column,
    slot_rows,
    select_t,
    stage,
    slots,
    earlier,
    unpack,
    mid,
    fin,
    rows,
    row_facts,
    outs,
    peer,
    sums,
    spread,
    back,
    partial_sum,
    ring_in,
    ring_out,
    load_sem,
    send_sem,
    recv_sem,
):
    grp, dev = lax.axis_index("grp"), lax.axis_index("dev")
    x, z = grp // NZ, lax.rem(grp, NZ)
    y, c = dev // 2, lax.rem(dev, 2)
    z_next = (x * NZ + lax.rem(z + 1, NZ), dev)
    z_prev = (x * NZ + lax.rem(z + NZ - 1, NZ), dev)
    x_next = (lax.rem(x + 1, NX) * NZ + z, dev)
    x_prev = (lax.rem(x + NX - 1, NX) * NZ + z, dev)
    y_next = (grp, lax.rem(y + 1, NY) * 2 + c)
    y_prev = (grp, lax.rem(y + NY - 1, NY) * 2 + c)
    twin = (grp, y * 2 + 1 - c)
    x_far = (lax.rem(x + 2, NX) * NZ + z, dev)

    load1 = pltpu.make_async_copy(w1_hbm.at[0], w1, load_sem.at[0])
    load2 = pltpu.make_async_copy(w2_hbm.at[0], w2, load_sem.at[1])
    load1.start()
    load2.start()

    barrier = pltpu.get_barrier_semaphore()
    for neighbour in (z_next, z_prev, x_next, x_prev, x_far, y_next, y_prev, twin):
        pl.semaphore_signal(barrier, inc=1, device_id=neighbour, device_id_type=MESH)
    pl.semaphore_wait(barrier, 8)

    started = []

    def send(src, dst, to):
        k = len(started)
        copy = pltpu.make_async_remote_copy(
            src_ref=src,
            dst_ref=dst,
            send_sem=send_sem.at[k],
            recv_sem=recv_sem.at[k],
            device_id=to,
            device_id_type=MESH,
        )
        copy.start()
        started.append(copy)
        return copy

    def block(r, h):
        at = ORDER.index(r if -7 <= r <= 8 else r % NZ)
        return column.at[pl.ds(at * TOK + h * PIECE, PIECE)]

    def pass_on(step, before):
        made = {}
        for h in range(PIECES):
            for way, to in ((1, z_next), (-1, z_prev)):
                if (h, way) in before:
                    before[h, way].wait_recv()
                if step > 8 or step == 8 and (h < PIECES // 2) == (way < 0):
                    continue
                held = -way * (step - 1)
                src = tok_ref.at[pl.ds(h * PIECE, PIECE)] if step == 1 else block(held, h)
                made[h, way] = send(src, block(held - way, h), to)
        return made

    tokens_in = pass_on(1, {})
    column[0:TOK, :] = tok_ref[...]

    lane_256 = iota((256, 256), 1)
    row_256 = iota((256, 256), 0)
    before_in_owner = ones_where(
        (row_256 < lane_256)
        & (lax.shift_right_logical(row_256, 6) == lax.shift_right_logical(lane_256, 6))
    )
    first_lanes = ones_where(iota((8, 128), 0) == iota((8, 128), 1))
    slot_base = (lax.shift_right_logical(iota((8, 256), 1), 6) * SLOT).astype(F32)
    slot_id = iota((QUAD, 256), 0).astype(F32)
    index_8 = iota((8, 256), 0)
    eye_rows = ones_where(row_256 == lane_256)
    x_ways = ((1, x_next, 3), (2, x_far, 2), (3, x_prev, 1))

    def quad(q, i):
        return pl.ds((q * NX + i) * QUAD, QUAD)

    def place_batch(q):
        at = slice(q * 256, q * 256 + 256)
        group_of = lax.dot_general(
            first_lanes, column[at, D:WIDE], NT, preferred_element_type=F32
        )
        hits = jnp.zeros((8, 256), F32)
        for i in range(NX):
            target = (lax.rem(x + i, NX) * NZ + z + 1).astype(F32)
            same = jnp.where(group_of == target, 1.0, 0.0)
            hit = same[0:1] + same[1:2] + same[2:3] + same[3:4]
            hits = jnp.where(index_8 == i, hit, hits)
        rank = mm(hits.astype(BF16), before_in_owner)
        slot = jnp.where(hits > 0, rank + slot_base, -1.0)
        slot_rows[q] = slot
        select = jnp.concatenate(
            [ones_where(slot_id == slot[i : i + 1]) for i in range(NX)], axis=0
        )
        got = mm(select, column[at, :]).astype(BF16)
        stage[q] = got
        slots[(q * NX) * QUAD : (q * NX) * QUAD + QUAD, :] = got[0:QUAD]
        return [
            send(stage.at[q, pl.ds(i * QUAD, QUAD)], slots.at[quad(q, there)], to)
            for i, to, there in (x_ways[1], x_ways[0], x_ways[2])
        ]

    def place_back(q):
        slot_t = lax.dot_general(
            eye_rows, slot_rows[q].astype(BF16), NT, preferred_element_type=F32
        )
        lane = iota((256, NX * QUAD), 1).astype(F32)
        hot = jnp.zeros((256, NX * QUAD), F32)
        for i in range(NX):
            col = slot_t[:, i : i + 1]
            hot = jnp.where((lane == col + float(i * QUAD)) & (col >= 0), 1.0, hot)
        select_t[q] = hot.astype(BF16)

    slots_in = []
    for step in range(2, 10):
        tokens_in = pass_on(step, tokens_in)
        if step == 2:
            for b in range(NX * NX * QUAD // 128):
                shape = (128, NX * NX * QUAD)
                earlier[b * 128 : (b + 1) * 128, :] = ones_where(
                    iota(shape, 1) < iota(shape, 0) + b * 128
                )
        if step in (3, 5, 7, 9):
            slots_in += place_batch(step // 2 - 1)
        if step in (4, 6, 8):
            place_back(step // 2 - 2)
    place_back(3)
    for copy in slots_in:
        copy.wait_recv()

    lane_r, lane_c = iota((128, 128), 0), iota((128, 128), 1)
    meta = slots[:, D:WIDE]
    lanes = iota((NX * NX * QUAD, 128), 1)
    match = ones_where((meta.astype(F32) == (grp + 1).astype(F32)) & (lanes < 4))
    repeat = ones_where((jnp.bitwise_and(lane_c, 3) == lane_r) & (lane_c < 20))
    live = mm(match, ones_where(lane_r < 4))
    chosen = (mm(match, repeat) * meta.astype(F32)).astype(BF16)
    facts = mm(
        chosen, ones_where((lax.shift_right_logical(lane_r, 2) == lane_c + 1) & (lane_r < 20))
    ).astype(BF16)
    place = jnp.where(live > 0, mm(earlier[...], live.astype(BF16)), -1.0)
    lane_f = lanes.astype(F32)
    unpack[:, 0:128] = ones_where(place == lane_f)
    unpack[:, 128:256] = ones_where(place == lane_f + 128.0)
    place_t = lax.dot_general(
        ones_where(iota((8, 128), 1) == 0), place.astype(BF16), NT, preferred_element_type=F32
    )
    pack = ones_where(iota((CAP, NX * NX * QUAD), 0).astype(F32) == place_t[0:1])
    rows[0, 0] = mm(pack, slots[:, 0:D]).astype(BF16)
    row_facts[0, 0] = lax.dot_general(
        first_lanes, mm(pack, facts).astype(BF16), NT, preferred_element_type=F32
    )

    def top(r):
        return pl.ds(r * 128, 128)

    def reduce_first(buf, nxt, prv):
        return (
            [send(buf.at[2, 0, top(r)], mid.at[0, top(r)], prv) for r in range(2)],
            [send(buf.at[2, 1, top(r)], mid.at[1, top(r)], nxt) for r in range(2)],
        )

    def reduce_direct(buf, i, nxt, prv):
        if i == 3:
            return [send(buf.at[3, 1, top(r)], fin.at[0, 1, top(r)], prv) for r in range(2)]
        return [send(buf.at[1, 0, top(r)], fin.at[1, 0, top(r)], nxt) for r in range(2)]

    def reduce_merge(buf, firsts, nxt, prv):
        made = []
        for r in range(2):
            rr = slice(r * 128, (r + 1) * 128)
            firsts[0][r].wait_recv()
            buf[3, 0, rr, :] = (
                buf[3, 0, rr, :].astype(F32) + mid[0, rr, :].astype(F32)
            ).astype(BF16)
            made.append(send(buf.at[3, 0, top(r)], fin.at[0, 0, top(r)], prv))
            firsts[1][r].wait_recv()
            buf[1, 1, rr, :] = (
                buf[1, 1, rr, :].astype(F32) + mid[1, rr, :].astype(F32)
            ).astype(BF16)
            made.append(send(buf.at[1, 1, top(r)], fin.at[1, 1, top(r)], nxt))
        return made

    def reduce_sum(buf, h):
        return (
            buf[0, h].astype(F32) + fin[0, h].astype(F32) + fin[1, h].astype(F32)
        ).astype(BF16)

    up, down = [], []
    for r in range(2):
        up.append(send(rows.at[0, 0, top(r)], rows.at[3, 0, top(r)], y_next))
        down.append(send(rows.at[0, 0, top(1 - r)], rows.at[1, 0, top(1 - r)], y_prev))
    across = [send(rows.at[0, 0], rows.at[0, 1], twin), send(row_facts.at[0, 0], row_facts.at[0, 1], twin)]
    f_up = send(row_facts.at[0, 0], row_facts.at[3, 0], y_next)
    f_down = send(row_facts.at[0, 0], row_facts.at[1, 0], y_prev)

    expert = dev.astype(F32)

    def feed_forward(i):
        block_in = rows[i].reshape(2 * CAP, D)

        def part(n, total):
            lo = pl.multiple_of(n * 512, 512)
            hidden = jnp.maximum(mm(block_in, w1[:, pl.ds(lo, 512)]), 0.0).astype(BF16)
            return total + mm(hidden, w2[pl.ds(lo, 512), :])

        total = lax.fori_loop(0, FF // 512, part, jnp.zeros((2 * CAP, D), F32))
        for core in range(2):
            f = row_facts[i, core]
            weight = jnp.where(f[0:1] == expert, f[2:3], 0.0) + jnp.where(f[1:2] == expert, f[3:4], 0.0)
            weight = jnp.broadcast_to(weight, (128, CAP)).astype(BF16)
            weight = lax.dot_general(eye_rows, weight, NT, preferred_element_type=F32)
            for n in range(6):
                outs[core, i, n // 3, :, (n % 3) * 128 : (n % 3 + 1) * 128] = (
                    total[core * CAP : (core + 1) * CAP, n * 128 : (n + 1) * 128] * weight
                ).astype(BF16)
        return send(outs.at[1, i], peer.at[i], twin)

    def join_cores(i, copy):
        copy.wait_recv()
        for h in range(2):
            outs[0, i, h] = (outs[0, i, h].astype(F32) + peer[i, h].astype(F32)).astype(BF16)

    load1.wait()
    load2.wait()
    for copy in across:
        copy.wait_recv()
    joins = {0: feed_forward(0)}
    far = []
    up[0].wait_recv()
    far.append(send(rows.at[3, 0, top(0)], rows.at[2, 0, top(0)], y_next))
    down[0].wait_recv()
    far.append(send(rows.at[1, 0, top(1)], rows.at[2, 0, top(1)], y_prev))
    f_up.wait_recv()
    far.append(send(row_facts.at[3, 0], row_facts.at[2, 0], y_next))
    up[1].wait_recv()
    across = {3: [send(rows.at[3, 0], rows.at[3, 1], twin), send(row_facts.at[3, 0], row_facts.at[3, 1], twin)]}
    down[1].wait_recv()
    f_down.wait_recv()
    across[1] = [send(rows.at[1, 0], rows.at[1, 1], twin), send(row_facts.at[1, 0], row_facts.at[1, 1], twin)]
    yn, yp = y_next, y_prev
    out_own = outs.at[0]
    for copy in across[3]:
        copy.wait_recv()
    joins[3] = feed_forward(3)
    for copy in far:
        copy.wait_recv()
    across[2] = [send(rows.at[2, 0], rows.at[2, 1], twin), send(row_facts.at[2, 0], row_facts.at[2, 1], twin)]
    join_cores(3, joins[3])
    finals = reduce_direct(out_own, 3, yn, yp)
    for copy in across[1]:
        copy.wait_recv()
    joins[1] = feed_forward(1)
    for copy in across[2]:
        copy.wait_recv()
    join_cores(1, joins[1])
    finals += reduce_direct(out_own, 1, yn, yp)
    joins[2] = feed_forward(2)
    join_cores(2, joins[2])
    firsts = reduce_first(out_own, yn, yp)
    join_cores(0, joins[0])
    finals += reduce_merge(out_own, firsts, yn, yp)
    for copy in finals:
        copy.wait_recv()
    for h in range(2):
        sums[:, h * HALF : (h + 1) * HALF] = reduce_sum(out_own, h)

    back_in = {}
    for q in range(NX - 1, -1, -1):
        at = slice(q * NX * QUAD, (q + 1) * NX * QUAD)
        got = mm(unpack[at, :], sums[...]).astype(BF16)
        spread[q] = got
        back[q, 0:QUAD, :] = got[0:QUAD]
        back_in[q] = [
            send(spread.at[q, pl.ds(i * QUAD, QUAD)], back.at[q, pl.ds(there * QUAD, QUAD)], to)
            for i, to, there in (x_ways[1], x_ways[0], x_ways[2])
        ]

    ready = set()

    def own_part(r, h):
        at = ORDER.index(r)
        q = at // 4
        if q not in ready:
            ready.add(q)
            for copy in back_in[q]:
                copy.wait_recv()
            partial_sum[q * 256 : (q + 1) * 256, :] = mm(select_t[q], back[q])
        return partial_sum[at * TOK + h * PIECE : at * TOK + (h + 1) * PIECE, :]

    arrived = {}
    for step in range(1, 9):
        current = {}
        for h in range(PIECES):
            part = pl.ds(h * PIECE, PIECE)
            for w, way, to in ((0, -1, z_prev), (1, 1, z_next)):
                if step == 1 and (h < PIECES // 2) != (w == 0):
                    continue
                value = own_part(8 if step == 1 else way * (9 - step), h)
                if (w, h) in arrived:
                    arrived[w, h].wait_recv()
                    value = value + ring_in[w, step - 2, h * PIECE : (h + 1) * PIECE, :].astype(F32)
                ring_out[w, step - 1, h * PIECE : (h + 1) * PIECE, :] = value.astype(BF16)
                current[w, h] = send(ring_out.at[w, step - 1, part], ring_in.at[w, step - 1, part], to)
        arrived = current
    for copy in arrived.values():
        copy.wait_recv()
    out_ref[...] = (
        partial_sum[0:TOK, :] + ring_in[0, 7].astype(F32) + ring_in[1, 7].astype(F32)
    ).astype(BF16)

    for copy in started:
        copy.wait_send()


def per_device(tokens, expert_ids, gates, w_in, w_out):
    pairs = expert_ids.reshape(TOK, 4, 2)
    gate_pairs = gates.reshape(TOK, 4, 2)
    tokens = jnp.concatenate(
        [
            tokens,
            (pairs[:, :, 0] // 8 + 1).astype(BF16),
            (pairs[:, :, 0] % 8).astype(BF16),
            (pairs[:, :, 1] % 8).astype(BF16),
            gate_pairs[:, :, 0],
            gate_pairs[:, :, 1],
            jnp.zeros((TOK, 108), BF16),
        ],
        axis=1,
    )
    vmem = pl.BlockSpec(memory_space=pltpu.VMEM)
    hbm = pl.BlockSpec(memory_space=pl.ANY)
    return pl.pallas_call(
        kernel,
        out_shape=jax.ShapeDtypeStruct((TOK, D), BF16),
        in_specs=[vmem, hbm, hbm],
        out_specs=vmem,
        scratch_shapes=[
            pltpu.VMEM((D, FF), BF16),
            pltpu.VMEM((FF, D), BF16),
            pltpu.VMEM((NZ * TOK, WIDE), BF16),
            pltpu.VMEM((NX, 8, 256), F32),
            pltpu.VMEM((NX, 256, NX * QUAD), BF16),
            pltpu.VMEM((NX, NX * QUAD, WIDE), BF16),
            pltpu.VMEM((NX * NX * QUAD, WIDE), BF16),
            pltpu.VMEM((NX * NX * QUAD, NX * NX * QUAD), BF16),
            pltpu.VMEM((NX * NX * QUAD, CAP), BF16),
            pltpu.VMEM((2, CAP, HALF), BF16),
            pltpu.VMEM((2, 2, CAP, HALF), BF16),
            pltpu.VMEM((4, 2, CAP, D), BF16),
            pltpu.VMEM((4, 2, 8, CAP), F32),
            pltpu.VMEM((2, 4, 2, CAP, HALF), BF16),
            pltpu.VMEM((4, 2, CAP, HALF), BF16),
            pltpu.VMEM((CAP, D), BF16),
            pltpu.VMEM((NX, NX * QUAD, D), BF16),
            pltpu.VMEM((NX, NX * QUAD, D), BF16),
            pltpu.VMEM((NZ * TOK, D), F32),
            pltpu.VMEM((2, 8, TOK, D), BF16),
            pltpu.VMEM((2, 8, TOK, D), BF16),
            pltpu.SemaphoreType.DMA((2,)),
            pltpu.SemaphoreType.DMA((COPIES,)),
            pltpu.SemaphoreType.DMA((COPIES,)),
        ],
        compiler_params=pltpu.CompilerParams(
            collective_id=0, has_side_effects=True, vmem_limit_bytes=56 * 1024 * 1024
        ),
        cost_estimate=pl.CostEstimate(
            flops=15_000_000_000, bytes_accessed=5_000_000, transcendentals=0
        ),
    )(tokens, w_in, w_out)


def solution(mesh):
    tok = P(("grp", "dev"), None)
    return jax.shard_map(
        per_device,
        mesh=mesh,
        in_specs=(tok, tok, tok, P(("grp", "dev"), None, None), P(("grp", "dev"), None, None)),
        out_specs=tok,
        check_vma=False,
    )
```

```python
import jax
import jax.numpy as jnp
from jax import lax
from jax.experimental import pallas as pl
from jax.experimental.pallas import tpu as pltpu
from jax.sharding import PartitionSpec as P

F32 = jnp.float32
BF16 = jnp.bfloat16
NX = 4
NY = 4
NZ = 16
TOK = 64
D = 768
FF = 1536
HIDE = 512
CAP = 256
WIDE = 896
SLOT = 12
QUAD = 48
COPIES = 240
PIECES = 4
PIECE = 16
BATCHES = ((0, 4, 48), (4, 4, 48), (8, 4, 48), (12, 3, 48), (15, 1, 16))
BULK = 768
SLOTS = 832
ORDER = (0, 1, -1, 2, -2, 3, -3, 4, -4, 5, -5, 6, -6, 7, -7, 8)
MESH = pl.DeviceIdType.MESH
NT = (((1,), (1,)), ((), ()))


def iota(shape, dim):
    return lax.broadcasted_iota(jnp.int32, shape, dim)


def ones_where(cond):
    return jnp.where(cond, 1.0, 0.0).astype(BF16)


def mm(a, b):
    return jnp.dot(a, b, preferred_element_type=F32)


def kernel(
    tok_ref,
    ids_ref,
    gates_ref,
    w1_hbm,
    w2_hbm,
    out_ref,
    w1,
    w2,
    column,
    slot_rows,
    select_t,
    stage,
    slots,
    earlier,
    unpack,
    fin,
    lhs,
    hid,
    gain,
    rows,
    row_facts,
    outs,
    peer,
    sums,
    spread,
    back,
    partial_sum,
    ring_in,
    ring_out,
    load_sem,
    send_sem,
    recv_sem,
):
    grp, dev = lax.axis_index("grp"), lax.axis_index("dev")
    x, z = grp // NZ, lax.rem(grp, NZ)
    y, c = dev // 2, lax.rem(dev, 2)
    z_next = (x * NZ + lax.rem(z + 1, NZ), dev)
    z_prev = (x * NZ + lax.rem(z + NZ - 1, NZ), dev)
    x_next = (lax.rem(x + 1, NX) * NZ + z, dev)
    x_prev = (lax.rem(x + NX - 1, NX) * NZ + z, dev)
    y_next = (grp, lax.rem(y + 1, NY) * 2 + c)
    y_prev = (grp, lax.rem(y + NY - 1, NY) * 2 + c)
    twin = (grp, y * 2 + 1 - c)
    y_far = (grp, lax.rem(y + 2, NY) * 2 + c)
    x_far = (lax.rem(x + 2, NX) * NZ + z, dev)

    load1 = pltpu.make_async_copy(w1_hbm.at[0], w1, load_sem.at[0])
    load2 = pltpu.make_async_copy(w2_hbm.at[0], w2, load_sem.at[1])
    load1.start()
    load2.start()

    barrier = pltpu.get_barrier_semaphore()
    for neighbour in (z_next, z_prev, x_next, x_prev, x_far, y_next, y_prev, y_far, twin):
        pl.semaphore_signal(barrier, inc=1, device_id=neighbour, device_id_type=MESH)

    ids = ids_ref[...]
    to_r, to_c = iota((8, 128), 0), iota((8, 128), 1)
    column[0:TOK, 0:D] = tok_ref[...]
    column[0:TOK, D:WIDE] = (
        mm(
            (lax.shift_right_logical(ids, 3) + 1).astype(F32).astype(BF16),
            ones_where((to_r == 2 * to_c) & (to_c < 4)),
        )
        + mm(
            jnp.bitwise_and(ids, 7).astype(F32).astype(BF16),
            ones_where(
                ((to_r == 2 * (to_c - 4)) & (to_c < 8)) | ((to_r == 2 * (to_c - 8) + 1) & (to_c < 12))
            ),
        )
        + mm(
            gates_ref[...],
            ones_where(
                ((to_r == 2 * (to_c - 12)) & (to_c < 16)) | ((to_r == 2 * (to_c - 16) + 1) & (to_c < 20))
            ),
        )
    ).astype(BF16)
    pl.semaphore_wait(barrier, 9)

    started = []

    def send(src, dst, to):
        k = len(started)
        copy = pltpu.make_async_remote_copy(
            src_ref=src,
            dst_ref=dst,
            send_sem=send_sem.at[k],
            recv_sem=recv_sem.at[k],
            device_id=to,
            device_id_type=MESH,
        )
        copy.start()
        started.append(copy)
        return copy

    def block(r, h):
        at = ORDER.index(r if -7 <= r <= 8 else r % NZ)
        return column.at[pl.ds(at * TOK + h * PIECE, PIECE)]

    def pass_on(step, before):
        made = {}
        for h in range(PIECES):
            for way, to in ((1, z_next), (-1, z_prev)):
                if (h, way) in before:
                    before[h, way].wait_recv()
                if step > 8 or step == 8 and (h < PIECES // 2) == (way < 0):
                    continue
                held = -way * (step - 1)
                made[h, way] = send(block(held, h), block(held - way, h), to)
        return made

    tokens_in = pass_on(1, {})
    first_lanes = ones_where(iota((8, 128), 0) == iota((8, 128), 1))
    x_ways = ((2, x_far, 2), (1, x_next, 3), (3, x_prev, 1))

    def eye(n):
        return ones_where(iota((n, n), 0) == iota((n, n), 1))

    def place_batch(q):
        at, owners, part = BATCHES[q]
        n = owners * TOK
        tokens = slice(at * TOK, at * TOK + n)
        group_of = lax.dot_general(
            first_lanes, column[tokens, D:WIDE], NT, preferred_element_type=F32
        )
        hits = jnp.zeros((8, n), F32)
        for i in range(NX):
            target = (lax.rem(x + i, NX) * NZ + z + 1).astype(F32)
            same = jnp.where(group_of == target, 1.0, 0.0)
            hit = same[0:1] + same[1:2] + same[2:3] + same[3:4]
            hits = jnp.where(iota((8, n), 0) == i, hit, hits)
        r, l = iota((n, n), 0), iota((n, n), 1)
        before = ones_where(
            (r < l) & (lax.shift_right_logical(r, 6) == lax.shift_right_logical(l, 6))
        )
        base = (lax.shift_right_logical(iota((8, n), 1), 6) * SLOT).astype(F32)
        slot = jnp.where(hits > 0, mm(hits.astype(BF16), before) + base, -1.0)
        slot_rows[q, :, 0:n] = slot
        slot_id = iota((part, n), 0).astype(F32)
        select = jnp.concatenate(
            [ones_where(slot_id == slot[i : i + 1]) for i in range(NX)], axis=0
        )
        got = mm(select, column[tokens, :]).astype(BF16)
        stage[q, 0 : NX * part, :] = got
        lo = q * NX * QUAD
        slots[lo : lo + part, :] = got[0:part]
        return [
            send(
                stage.at[q, pl.ds(i * part, part)], slots.at[pl.ds(lo + there * part, part)], to
            )
            for i, to, there in x_ways
        ]

    def place_back(q):
        owners, part = BATCHES[q][1:]
        n = owners * TOK
        slot_t = lax.dot_general(
            eye(n), slot_rows[q, :, 0:n].astype(BF16), NT, preferred_element_type=F32
        )
        lane = iota((n, NX * part), 1).astype(F32)
        hot = jnp.zeros((n, NX * part), F32)
        for i in range(NX):
            col = slot_t[:, i : i + 1]
            hot = jnp.where((lane == col + float(i * part)) & (col >= 0), 1.0, hot)
        select_t[q, 0:n, 0 : NX * part] = hot.astype(BF16)

    slots_in = {}
    for step in range(2, 10):
        tokens_in = pass_on(step, tokens_in)
        if step == 2:
            for b in range(BULK // 128):
                shape = (128, BULK)
                earlier[b * 128 : (b + 1) * 128, :] = ones_where(
                    iota(shape, 1) < iota(shape, 0) + b * 128
                )
        if step in (3, 5, 7, 8, 9):
            q = (3, 5, 7, 8, 9).index(step)
            slots_in[q] = place_batch(q)
        if step in (4, 6):
            place_back(step // 2 - 2)
    place_back(2)
    for q in range(4):
        for copy in slots_in[q]:
            copy.wait_recv()

    lane_r, lane_c = iota((128, 128), 0), iota((128, 128), 1)
    repeat = ones_where((jnp.bitwise_and(lane_c, 3) == lane_r) & (lane_c < 20))
    first_four = ones_where(lane_r < 4)
    to_facts = ones_where((lax.shift_right_logical(lane_r, 2) == lane_c + 1) & (lane_r < 20))

    def read_slots(lo, n):
        meta = slots[lo : lo + n, D:WIDE].astype(F32)
        match = ones_where((meta == (grp + 1).astype(F32)) & (iota((n, 128), 1) < 4))
        chosen = (mm(match, repeat) * meta).astype(BF16)
        return mm(match, first_four), mm(chosen, to_facts).astype(BF16)

    def pack_slots(lo, n, place, facts):
        lane_f = iota((n, 128), 1).astype(F32)
        unpack[lo : lo + n, 0:128] = ones_where(place == lane_f)
        unpack[lo : lo + n, 128:256] = ones_where(place == lane_f + 128.0)
        place_t = lax.dot_general(
            ones_where(iota((8, 128), 1) == 0), place.astype(BF16), NT, preferred_element_type=F32
        )
        pack = ones_where(iota((CAP, n), 0).astype(F32) == place_t[0:1])
        return mm(pack, slots[lo : lo + n, 0:D]), mm(pack, facts)

    live, facts = read_slots(0, BULK)
    live_b = live.astype(BF16)
    place = jnp.where(live > 0, mm(earlier[...], live_b), -1.0)
    bulk_rows, bulk_facts = pack_slots(0, BULK, place, facts)
    bulk_count = mm(ones_where(iota((SLOTS - BULK, BULK), 0) >= 0), live_b)
    place_back(3)
    place_back(4)
    for copy in slots_in[4]:
        copy.wait_recv()
    live, facts = read_slots(BULK, SLOTS - BULK)
    shape = (SLOTS - BULK, SLOTS - BULK)
    place = bulk_count + mm(ones_where(iota(shape, 1) < iota(shape, 0)), live.astype(BF16))
    place = jnp.where(live > 0, place, -1.0)
    last_rows, last_facts = pack_slots(BULK, SLOTS - BULK, place, facts)
    rows[0, 0] = (bulk_rows + last_rows).astype(BF16)
    row_facts[0, 0] = lax.dot_general(
        first_lanes, (bulk_facts + last_facts).astype(BF16), NT, preferred_element_type=F32
    )

    def top(r):
        return pl.ds(r * 128, 128)

    f_up = send(row_facts.at[0, 0], row_facts.at[3, 0], y_next)
    f_down = send(row_facts.at[0, 0], row_facts.at[1, 0], y_prev)
    up, down = [], []
    for r in range(2):
        up.append(send(rows.at[0, 0, top(r)], rows.at[3, 0, top(r)], y_next))
        down.append(send(rows.at[0, 0, top(1 - r)], rows.at[1, 0, top(1 - r)], y_prev))

    def rows_across(i, r):
        return send(rows.at[i, 0, top(r)], rows.at[i, 1, top(r)], twin)

    def facts_across(i):
        return send(row_facts.at[i, 0], row_facts.at[i, 1], twin)

    expert = dev.astype(F32)
    eye_rows = eye(CAP)

    def gains(i):
        for core in range(2):
            f = row_facts[i, core]
            weight = jnp.where(f[0:1] == expert, f[2:3], 0.0) + jnp.where(f[1:2] == expert, f[3:4], 0.0)
            weight = jnp.broadcast_to(weight, (128, CAP)).astype(BF16)
            gain[i, core] = lax.dot_general(eye_rows, weight, NT, preferred_element_type=F32)

    def into_hidden(parts):
        for m, (i, core, r) in enumerate(parts):
            lhs[m * 128 : (m + 1) * 128, :] = rows[i, core, r * 128 : (r + 1) * 128, :]

        def part(n, carry):
            at = pl.ds(pl.multiple_of(n * HIDE, HIDE), HIDE)
            hid[:, at] = jnp.maximum(mm(lhs[...], w1[:, at]), 0.0).astype(BF16)
            return carry

        lax.fori_loop(0, FF // HIDE, part, 0)

    def from_hidden(parts, lo=0):
        def part(n, carry):
            at = pl.ds(pl.multiple_of(n * 256, 256), 256)
            got = mm(hid[lo : lo + len(parts) * 128, :], w2[:, at])
            for m, (i, core, r) in enumerate(parts):
                weight = gain[i, core, r * 128 : (r + 1) * 128, :]
                outs[core, i, r * 128 : (r + 1) * 128, at] = (
                    got[m * 128 : (m + 1) * 128] * jnp.concatenate([weight, weight], axis=1)
                ).astype(BF16)
            return carry

        lax.fori_loop(0, D // 256, part, 0)
        return {
            (i, r): send(outs.at[1, i, top(r)], peer.at[i, top(r)], twin)
            for i, core, r in parts
            if core
        }

    y_ways = {1: (y_next, 3), 2: (y_far, 2), 3: (y_prev, 1)}
    finals = []

    def join_cores(i, r, copy):
        copy.wait_recv()
        rr = slice(r * 128, (r + 1) * 128)
        outs[0, i, rr, :] = (outs[0, i, rr, :].astype(F32) + peer[i, rr, :].astype(F32)).astype(BF16)
        to, there = y_ways[i]
        finals.append(send(outs.at[0, i, top(r)], fin.at[there, top(r)], to))

    def both(*halves):
        return [(i, core, r) for core in (1, 0) for i, r in halves]

    near = both((0, 0), (0, 1))
    early = both((3, 0), (1, 1))
    late = both((3, 1), (1, 0))
    last = both((2, 0), (2, 1))
    waits = [rows_across(0, 0), rows_across(0, 1), facts_across(0)]
    load1.wait()
    load2.wait()
    for copy in waits:
        copy.wait_recv()
    gains(0)
    into_hidden(near)
    near_in = from_hidden(near)
    f_up.wait_recv()
    f_far = send(row_facts.at[3, 0], row_facts.at[2, 0], y_next)
    waits = [facts_across(3)]
    f_down.wait_recv()
    waits.append(facts_across(1))
    up[0].wait_recv()
    far = [send(rows.at[3, 0, top(0)], rows.at[2, 0, top(0)], y_next)]
    waits.append(rows_across(3, 0))
    down[0].wait_recv()
    far.append(send(rows.at[1, 0, top(1)], rows.at[2, 0, top(1)], y_prev))
    waits.append(rows_across(1, 1))
    for copy in waits:
        copy.wait_recv()
    gains(3)
    gains(1)
    into_hidden(early)
    early_in = from_hidden(early)
    up[1].wait_recv()
    waits = [rows_across(3, 1)]
    down[1].wait_recv()
    waits.append(rows_across(1, 0))
    f_far.wait_recv()
    waits.append(facts_across(2))
    for copy in waits:
        copy.wait_recv()
    into_hidden(late)
    for (i, r), copy in early_in.items():
        join_cores(i, r, copy)
    gains(2)
    waits = []
    for r in range(2):
        far[r].wait_recv()
        waits.append(rows_across(2, r))
    late_in = from_hidden(late)
    for copy in waits:
        copy.wait_recv()
    into_hidden(last)
    for (i, r), copy in late_in.items():
        join_cores(i, r, copy)
    last_in = from_hidden(last[:2])
    from_hidden(last[2:], CAP)
    for (i, r), copy in last_in.items():
        join_cores(i, r, copy)
    for copy in near_in.values():
        copy.wait_recv()
    own_sum = outs[0, 0].astype(F32) + peer[0].astype(F32)
    for copy in finals:
        copy.wait_recv()
    sums[...] = (
        own_sum + fin[1].astype(F32) + fin[2].astype(F32) + fin[3].astype(F32)
    ).astype(BF16)

    back_in = {}
    for q in range(len(BATCHES) - 1, -1, -1):
        part = BATCHES[q][2]
        lo = q * NX * QUAD
        got = mm(unpack[lo : lo + NX * part, :], sums[...]).astype(BF16)
        spread[q, 0 : NX * part, :] = got
        back[q, 0:part, :] = got[0:part]
        back_in[q] = [
            send(spread.at[q, pl.ds(i * part, part)], back.at[q, pl.ds(there * part, part)], to)
            for i, to, there in x_ways
        ]

    ready = set()

    def own_part(r, h):
        at = ORDER.index(r)
        q = min(at // 4, 3) if r != 8 else 4
        if q not in ready:
            ready.add(q)
            for copy in back_in[q]:
                copy.wait_recv()
            first, owners, part = BATCHES[q]
            n = owners * TOK
            partial_sum[first * TOK : first * TOK + n, :] = mm(
                select_t[q, 0:n, 0 : NX * part], back[q, 0 : NX * part, :]
            )
        return partial_sum[at * TOK + h * PIECE : at * TOK + (h + 1) * PIECE, :]

    arrived = {}
    for step in range(1, 9):
        current = {}
        for h in range(PIECES):
            part = pl.ds(h * PIECE, PIECE)
            for w, way, to in ((0, -1, z_prev), (1, 1, z_next)):
                if step == 1 and (h < PIECES // 2) != (w == 0):
                    continue
                value = own_part(8 if step == 1 else way * (9 - step), h)
                if (w, h) in arrived:
                    arrived[w, h].wait_recv()
                    value = value + ring_in[w, step - 2, h * PIECE : (h + 1) * PIECE, :].astype(F32)
                ring_out[w, step - 1, h * PIECE : (h + 1) * PIECE, :] = value.astype(BF16)
                current[w, h] = send(ring_out.at[w, step - 1, part], ring_in.at[w, step - 1, part], to)
        arrived = current
    for copy in arrived.values():
        copy.wait_recv()
    out_ref[...] = (
        partial_sum[0:TOK, :] + ring_in[0, 7].astype(F32) + ring_in[1, 7].astype(F32)
    ).astype(BF16)

    for copy in started:
        copy.wait_send()


def per_device(tokens, expert_ids, gates, w_in, w_out):
    vmem = pl.BlockSpec(memory_space=pltpu.VMEM)
    hbm = pl.BlockSpec(memory_space=pl.ANY)
    return pl.pallas_call(
        kernel,
        out_shape=jax.ShapeDtypeStruct((TOK, D), BF16),
        in_specs=[vmem, vmem, vmem, hbm, hbm],
        out_specs=vmem,
        scratch_shapes=[
            pltpu.VMEM((D, FF), BF16),
            pltpu.VMEM((FF, D), BF16),
            pltpu.VMEM((NZ * TOK, WIDE), BF16),
            pltpu.VMEM((5, 8, 256), F32),
            pltpu.VMEM((5, 256, NX * QUAD), BF16),
            pltpu.VMEM((5, NX * QUAD, WIDE), BF16),
            pltpu.VMEM((SLOTS, WIDE), BF16),
            pltpu.VMEM((BULK, BULK), BF16),
            pltpu.VMEM((SLOTS, CAP), BF16),
            pltpu.VMEM((4, CAP, D), BF16),
            pltpu.VMEM((2 * CAP, D), BF16),
            pltpu.VMEM((2 * CAP, FF), BF16),
            pltpu.VMEM((4, 2, CAP, 128), F32),
            pltpu.VMEM((4, 2, CAP, D), BF16),
            pltpu.VMEM((4, 2, 8, CAP), F32),
            pltpu.VMEM((2, 4, CAP, D), BF16),
            pltpu.VMEM((4, CAP, D), BF16),
            pltpu.VMEM((CAP, D), BF16),
            pltpu.VMEM((5, NX * QUAD, D), BF16),
            pltpu.VMEM((5, NX * QUAD, D), BF16),
            pltpu.VMEM((NZ * TOK, D), F32),
            pltpu.VMEM((2, 8, TOK, D), BF16),
            pltpu.VMEM((2, 8, TOK, D), BF16),
            pltpu.SemaphoreType.DMA((2,)),
            pltpu.SemaphoreType.DMA((COPIES,)),
            pltpu.SemaphoreType.DMA((COPIES,)),
        ],
        compiler_params=pltpu.CompilerParams(
            collective_id=0, has_side_effects=True, vmem_limit_bytes=56 * 1024 * 1024
        ),
        cost_estimate=pl.CostEstimate(
            flops=15_000_000_000, bytes_accessed=5_000_000, transcendentals=0
        ),
    )(tokens, expert_ids, gates, w_in, w_out)


def solution(mesh):
    tok = P(("grp", "dev"), None)
    return jax.shard_map(
        per_device,
        mesh=mesh,
        in_specs=(tok, tok, tok, P(("grp", "dev"), None, None), P(("grp", "dev"), None, None)),
        out_specs=tok,
        check_vma=False,
    )
```

```python
import jax
import jax.numpy as jnp
from jax import lax
from jax.experimental import pallas as pl
from jax.experimental.pallas import tpu as pltpu
from jax.sharding import PartitionSpec as P

F32 = jnp.float32
BF16 = jnp.bfloat16
NX = 4
NY = 4
NZ = 16
TOK = 64
D = 768
FF = 1536
HIDE = 512
CAP = 256
WIDE = 896
SLOT = 12
QUAD = 48
COPIES = 240
PIECES = 4
PIECE = 16
BATCHES = ((0, 4, 48), (4, 4, 48), (8, 4, 48), (12, 3, 48), (15, 1, 16))
BULK = 768
SLOTS = 832
ORDER = (0, 1, -1, 2, -2, 3, -3, 4, -4, 5, -5, 6, -6, 7, -7, 8)
MESH = pl.DeviceIdType.MESH
NT = (((1,), (1,)), ((), ()))


def iota(shape, dim):
    return lax.broadcasted_iota(jnp.int32, shape, dim)


def ones_where(cond):
    return jnp.where(cond, 1.0, 0.0).astype(BF16)


def mm(a, b):
    return jnp.dot(a, b, preferred_element_type=F32)


def kernel(
    tok_ref,
    ids_ref,
    gates_ref,
    w1_hbm,
    w2_hbm,
    out_ref,
    w1,
    w2,
    column,
    slot_rows,
    select_t,
    stage,
    slots,
    earlier,
    unpack,
    fin,
    lhs,
    hid,
    gain,
    rows,
    row_facts,
    outs,
    peer,
    sums,
    spread,
    back,
    partial_sum,
    ring_in,
    ring_out,
    load_sem,
    send_sem,
    recv_sem,
):
    grp, dev = lax.axis_index("grp"), lax.axis_index("dev")
    x, z = grp // NZ, lax.rem(grp, NZ)
    y, c = dev // 2, lax.rem(dev, 2)
    z_next = (x * NZ + lax.rem(z + 1, NZ), dev)
    z_prev = (x * NZ + lax.rem(z + NZ - 1, NZ), dev)
    x_next = (lax.rem(x + 1, NX) * NZ + z, dev)
    x_prev = (lax.rem(x + NX - 1, NX) * NZ + z, dev)
    y_next = (grp, lax.rem(y + 1, NY) * 2 + c)
    y_prev = (grp, lax.rem(y + NY - 1, NY) * 2 + c)
    twin = (grp, y * 2 + 1 - c)
    y_far = (grp, lax.rem(y + 2, NY) * 2 + c)
    x_far = (lax.rem(x + 2, NX) * NZ + z, dev)

    load1 = pltpu.make_async_copy(w1_hbm.at[0], w1, load_sem.at[0])
    load2 = pltpu.make_async_copy(w2_hbm.at[0], w2, load_sem.at[1])
    load1.start()
    load2.start()

    barrier = pltpu.get_barrier_semaphore()
    for neighbour in (z_next, z_prev, x_next, x_prev, x_far, y_next, y_prev, y_far, twin):
        pl.semaphore_signal(barrier, inc=1, device_id=neighbour, device_id_type=MESH)

    square_r, square_c = iota((TOK, TOK), 0), iota((TOK, TOK), 1)

    def turned(picks):
        return lax.dot_general(
            ones_where(square_r == square_c), picks, NT, preferred_element_type=F32
        ).astype(BF16)

    ids = ids_ref[...]
    to_r, to_c = iota((8, 128), 0), iota((8, 128), 1)
    column[0:TOK, 0:D] = tok_ref[...]
    column[0:TOK, D:WIDE] = (
        mm(
            turned((lax.shift_right_logical(ids, 3) + 1).astype(F32).astype(BF16)),
            ones_where((to_r == 2 * to_c) & (to_c < 4)),
        )
        + mm(
            turned(jnp.bitwise_and(ids, 7).astype(F32).astype(BF16)),
            ones_where(
                ((to_r == 2 * (to_c - 4)) & (to_c < 8)) | ((to_r == 2 * (to_c - 8) + 1) & (to_c < 12))
            ),
        )
        + mm(
            turned(gates_ref[...]),
            ones_where(
                ((to_r == 2 * (to_c - 12)) & (to_c < 16)) | ((to_r == 2 * (to_c - 16) + 1) & (to_c < 20))
            ),
        )
    ).astype(BF16)
    pl.semaphore_wait(barrier, 9)

    started = []
    numbers = iter(range(COPIES))

    def send(src, dst, to):
        k = next(numbers)
        copy = pltpu.make_async_remote_copy(
            src_ref=src,
            dst_ref=dst,
            send_sem=send_sem.at[k],
            recv_sem=recv_sem.at[k],
            device_id=to,
            device_id_type=MESH,
        )
        copy.start()
        started.append(copy)
        return copy

    def block(r, h):
        at = ORDER.index(r if -7 <= r <= 8 else r % NZ)
        return column.at[pl.ds(at * TOK + h * PIECE, PIECE)]

    def pass_on(step, before):
        made = {}
        for h in range(PIECES):
            for way, to in ((1, z_next), (-1, z_prev)):
                if (h, way) in before:
                    before[h, way].wait_recv()
                if step > 8 or step == 8 and (h < PIECES // 2) == (way < 0):
                    continue
                held = -way * (step - 1)
                made[h, way] = send(block(held, h), block(held - way, h), to)
        return made

    tokens_in = pass_on(1, {})
    first_lanes = ones_where(iota((8, 128), 0) == iota((8, 128), 1))
    x_ways = ((2, x_far, 2), (1, x_next, 3), (3, x_prev, 1))

    def eye(n):
        return ones_where(iota((n, n), 0) == iota((n, n), 1))

    def place_batch(q):
        at, owners, part = BATCHES[q]
        n = owners * TOK
        tokens = slice(at * TOK, at * TOK + n)
        group_of = lax.dot_general(
            first_lanes, column[tokens, D:WIDE], NT, preferred_element_type=F32
        )
        hits = jnp.zeros((8, n), F32)
        for i in range(NX):
            target = (lax.rem(x + i, NX) * NZ + z + 1).astype(F32)
            same = jnp.where(group_of == target, 1.0, 0.0)
            hit = same[0:1] + same[1:2] + same[2:3] + same[3:4]
            hits = jnp.where(iota((8, n), 0) == i, hit, hits)
        r, l = iota((n, n), 0), iota((n, n), 1)
        before = ones_where(
            (r < l) & (lax.shift_right_logical(r, 6) == lax.shift_right_logical(l, 6))
        )
        base = (lax.shift_right_logical(iota((8, n), 1), 6) * SLOT).astype(F32)
        slot = jnp.where(hits > 0, mm(hits.astype(BF16), before) + base, -1.0)
        slot_rows[q, :, 0:n] = slot
        slot_id = iota((part, n), 0).astype(F32)
        select = jnp.concatenate(
            [ones_where(slot_id == slot[i : i + 1]) for i in range(NX)], axis=0
        )
        got = mm(select, column[tokens, :]).astype(BF16)
        stage[q, 0 : NX * part, :] = got
        lo = q * NX * QUAD
        slots[lo : lo + part, :] = got[0:part]
        return [
            send(
                stage.at[q, pl.ds(i * part, part)], slots.at[pl.ds(lo + there * part, part)], to
            )
            for i, to, there in x_ways
        ]

    def place_back(q):
        owners, part = BATCHES[q][1:]
        n = owners * TOK
        slot_t = lax.dot_general(
            eye(n), slot_rows[q, :, 0:n].astype(BF16), NT, preferred_element_type=F32
        )
        lane = iota((n, NX * part), 1).astype(F32)
        hot = jnp.zeros((n, NX * part), F32)
        for i in range(NX):
            col = slot_t[:, i : i + 1]
            hot = jnp.where((lane == col + float(i * part)) & (col >= 0), 1.0, hot)
        select_t[q, 0:n, 0 : NX * part] = hot.astype(BF16)

    slots_in = {}
    for step in range(2, 10):
        tokens_in = pass_on(step, tokens_in)
        if step == 2:
            for b in range(BULK // 128):
                shape = (128, BULK)
                earlier[b * 128 : (b + 1) * 128, :] = ones_where(
                    iota(shape, 1) < iota(shape, 0) + b * 128
                )
        if step in (3, 5, 7, 8, 9):
            q = (3, 5, 7, 8, 9).index(step)
            slots_in[q] = place_batch(q)
        if step in (4, 6):
            place_back(step // 2 - 2)
    place_back(2)
    for q in range(4):
        for copy in slots_in[q]:
            copy.wait_recv()

    lane_r, lane_c = iota((128, 128), 0), iota((128, 128), 1)
    repeat = ones_where((jnp.bitwise_and(lane_c, 3) == lane_r) & (lane_c < 20))
    first_four = ones_where(lane_r < 4)
    to_facts = ones_where((lax.shift_right_logical(lane_r, 2) == lane_c + 1) & (lane_r < 20))

    def read_slots(lo, n):
        meta = slots[lo : lo + n, D:WIDE].astype(F32)
        match = ones_where((meta == (grp + 1).astype(F32)) & (iota((n, 128), 1) < 4))
        chosen = (mm(match, repeat) * meta).astype(BF16)
        return mm(match, first_four), mm(chosen, to_facts).astype(BF16)

    def pack_slots(lo, n, place, facts):
        lane_f = iota((n, 128), 1).astype(F32)
        unpack[lo : lo + n, 0:128] = ones_where(place == lane_f)
        unpack[lo : lo + n, 128:256] = ones_where(place == lane_f + 128.0)
        place_t = lax.dot_general(
            ones_where(iota((8, 128), 1) == 0), place.astype(BF16), NT, preferred_element_type=F32
        )
        pack = ones_where(iota((CAP, n), 0).astype(F32) == place_t[0:1])
        return mm(pack, slots[lo : lo + n, 0:D]), mm(pack, facts)

    live, facts = read_slots(0, BULK)
    live_b = live.astype(BF16)
    place = jnp.where(live > 0, mm(earlier[...], live_b), -1.0)
    bulk_rows, bulk_facts = pack_slots(0, BULK, place, facts)
    bulk_count = mm(ones_where(iota((SLOTS - BULK, BULK), 0) >= 0), live_b)
    place_back(3)
    place_back(4)
    for copy in slots_in[4]:
        copy.wait_recv()
    live, facts = read_slots(BULK, SLOTS - BULK)
    shape = (SLOTS - BULK, SLOTS - BULK)
    place = bulk_count + mm(ones_where(iota(shape, 1) < iota(shape, 0)), live.astype(BF16))
    place = jnp.where(live > 0, place, -1.0)
    last_rows, last_facts = pack_slots(BULK, SLOTS - BULK, place, facts)
    rows[0, 0] = (bulk_rows + last_rows).astype(BF16)
    row_facts[0, 0] = lax.dot_general(
        first_lanes, (bulk_facts + last_facts).astype(BF16), NT, preferred_element_type=F32
    )

    def top(r):
        return pl.ds(r * 128, 128)

    f_up = send(row_facts.at[0, 0], row_facts.at[3, 0], y_next)
    f_down = send(row_facts.at[0, 0], row_facts.at[1, 0], y_prev)
    up, down = [], []

    def along_y(r):
        up.append(send(rows.at[0, 0, top(r)], rows.at[3, 0, top(r)], y_next))
        down.append(send(rows.at[0, 0, top(1 - r)], rows.at[1, 0, top(1 - r)], y_prev))

    along_y(0)

    def rows_across(i, r):
        return send(rows.at[i, 0, top(r)], rows.at[i, 1, top(r)], twin)

    def facts_across(i):
        return send(row_facts.at[i, 0], row_facts.at[i, 1], twin)

    expert = dev.astype(F32)
    eye_rows = eye(CAP)

    def gains(i):
        for core in range(2):
            f = row_facts[i, core]
            weight = jnp.where(f[0:1] == expert, f[2:3], 0.0) + jnp.where(f[1:2] == expert, f[3:4], 0.0)
            weight = jnp.broadcast_to(weight, (128, CAP)).astype(BF16)
            gain[i, core] = lax.dot_general(eye_rows, weight, NT, preferred_element_type=F32)

    def into_hidden(parts):
        for m, (i, core, r) in enumerate(parts):
            lhs[m * 128 : (m + 1) * 128, :] = rows[i, core, r * 128 : (r + 1) * 128, :]

        def part(n, carry):
            at = pl.ds(pl.multiple_of(n * HIDE, HIDE), HIDE)
            hid[:, at] = jnp.maximum(mm(lhs[...], w1[:, at]), 0.0).astype(BF16)
            return carry

        lax.fori_loop(0, FF // HIDE, part, 0)

    def from_hidden(parts, lo=0):
        def part(n, carry):
            at = pl.ds(pl.multiple_of(n * 256, 256), 256)
            got = mm(hid[lo : lo + len(parts) * 128, :], w2[:, at])
            for m, (i, core, r) in enumerate(parts):
                weight = gain[i, core, r * 128 : (r + 1) * 128, :]
                outs[core, i, r * 128 : (r + 1) * 128, at] = (
                    got[m * 128 : (m + 1) * 128] * jnp.concatenate([weight, weight], axis=1)
                ).astype(BF16)
            return carry

        lax.fori_loop(0, D // 256, part, 0)
        return {
            (i, r): send(outs.at[1, i, top(r)], peer.at[i, top(r)], twin)
            for i, core, r in parts
            if core
        }

    y_ways = {1: (y_next, 3), 2: (y_far, 2), 3: (y_prev, 1)}
    finals = []

    def join_cores(i, r, copy):
        copy.wait_recv()
        rr = slice(r * 128, (r + 1) * 128)
        outs[0, i, rr, :] = (outs[0, i, rr, :].astype(F32) + peer[i, rr, :].astype(F32)).astype(BF16)
        to, there = y_ways[i]
        finals.append(send(outs.at[0, i, top(r)], fin.at[there, top(r)], to))

    def both(*halves):
        return [(i, core, r) for core in (1, 0) for i, r in halves]

    near = both((0, 0), (0, 1))
    early = both((3, 0), (1, 1))
    late = both((3, 1), (1, 0))
    last = both((2, 0), (2, 1))
    waits = [rows_across(0, 0), rows_across(0, 1), facts_across(0)]
    load1.wait()
    load2.wait()
    for copy in waits:
        copy.wait_recv()
    gains(0)
    into_hidden(near)
    for copy in (up[0], down[0]):
        copy.wait_send()
        started[:] = [other for other in started if other is not copy]
    along_y(1)
    near_in = from_hidden(near)
    f_up.wait_recv()
    f_far = send(row_facts.at[3, 0], row_facts.at[2, 0], y_next)
    waits = [facts_across(3)]
    f_down.wait_recv()
    waits.append(facts_across(1))
    for copy in waits:
        copy.wait_recv()
    gains(3)
    gains(1)
    waits = []
    up[0].wait_recv()
    far = [send(rows.at[3, 0, top(0)], rows.at[2, 0, top(0)], y_next)]
    waits.append(rows_across(3, 0))
    down[0].wait_recv()
    far.append(send(rows.at[1, 0, top(1)], rows.at[2, 0, top(1)], y_prev))
    waits.append(rows_across(1, 1))
    for copy in waits:
        copy.wait_recv()
    into_hidden(early)
    early_in = from_hidden(early)
    up[1].wait_recv()
    waits = [rows_across(3, 1)]
    down[1].wait_recv()
    waits.append(rows_across(1, 0))
    f_far.wait_recv()
    waits.append(facts_across(2))
    for copy in waits:
        copy.wait_recv()
    into_hidden(late)
    for (i, r), copy in early_in.items():
        join_cores(i, r, copy)
    gains(2)
    waits = []
    for r in range(2):
        far[r].wait_recv()
        waits.append(rows_across(2, r))
    late_in = from_hidden(late)
    for copy in waits:
        copy.wait_recv()
    into_hidden(last)
    for (i, r), copy in late_in.items():
        join_cores(i, r, copy)
    last_in = from_hidden(last[:2])
    from_hidden(last[2:], CAP)
    for (i, r), copy in last_in.items():
        join_cores(i, r, copy)
    for copy in near_in.values():
        copy.wait_recv()
    own_sum = outs[0, 0].astype(F32) + peer[0].astype(F32)
    for copy in finals:
        copy.wait_recv()
    sums[...] = (
        own_sum + fin[1].astype(F32) + fin[2].astype(F32) + fin[3].astype(F32)
    ).astype(BF16)

    back_in = {}

    def along_x(q):
        part = BATCHES[q][2]
        lo = q * NX * QUAD
        got = mm(unpack[lo : lo + NX * part, :], sums[...]).astype(BF16)
        spread[q, 0 : NX * part, :] = got
        back[q, 0:part, :] = got[0:part]
        back_in[q] = [
            send(spread.at[q, pl.ds(i * part, part)], back.at[q, pl.ds(there * part, part)], to)
            for i, to, there in x_ways
        ]

    along_x(4)
    along_x(3)
    ready = set()

    def own_part(r, h):
        at = ORDER.index(r)
        q = min(at // 4, 3) if r != 8 else 4
        if q not in ready:
            ready.add(q)
            for copy in back_in[q]:
                copy.wait_recv()
            first, owners, part = BATCHES[q]
            n = owners * TOK
            partial_sum[first * TOK : first * TOK + n, :] = mm(
                select_t[q, 0:n, 0 : NX * part], back[q, 0 : NX * part, :]
            )
        return partial_sum[at * TOK + h * PIECE : at * TOK + (h + 1) * PIECE, :]

    arrived = {}
    for step in range(1, 9):
        current = {}
        for h in range(PIECES):
            part = pl.ds(h * PIECE, PIECE)
            for w, way, to in ((0, -1, z_prev), (1, 1, z_next)):
                if step == 1 and (h < PIECES // 2) != (w == 0):
                    continue
                value = own_part(8 if step == 1 else way * (9 - step), h)
                if (w, h) in arrived:
                    arrived[w, h].wait_recv()
                    value = value + ring_in[w, step - 2, h * PIECE : (h + 1) * PIECE, :].astype(F32)
                ring_out[w, step - 1, h * PIECE : (h + 1) * PIECE, :] = value.astype(BF16)
                current[w, h] = send(ring_out.at[w, step - 1, part], ring_in.at[w, step - 1, part], to)
        arrived = current
        if step in (1, 2, 4):
            along_x({1: 2, 2: 1, 4: 0}[step])
    for copy in arrived.values():
        copy.wait_recv()
    out_ref[...] = (
        partial_sum[0:TOK, :] + ring_in[0, 7].astype(F32) + ring_in[1, 7].astype(F32)
    ).astype(BF16)

    for copy in started:
        copy.wait_send()


def per_device(tokens, expert_ids, gates, w_in, w_out):
    vmem = pl.BlockSpec(memory_space=pltpu.VMEM)
    hbm = pl.BlockSpec(memory_space=pl.ANY)
    return pl.pallas_call(
        kernel,
        out_shape=jax.ShapeDtypeStruct((TOK, D), BF16),
        in_specs=[vmem, vmem, vmem, hbm, hbm],
        out_specs=vmem,
        scratch_shapes=[
            pltpu.VMEM((D, FF), BF16),
            pltpu.VMEM((FF, D), BF16),
            pltpu.VMEM((NZ * TOK, WIDE), BF16),
            pltpu.VMEM((5, 8, 256), F32),
            pltpu.VMEM((5, 256, NX * QUAD), BF16),
            pltpu.VMEM((5, NX * QUAD, WIDE), BF16),
            pltpu.VMEM((SLOTS, WIDE), BF16),
            pltpu.VMEM((BULK, BULK), BF16),
            pltpu.VMEM((SLOTS, CAP), BF16),
            pltpu.VMEM((4, CAP, D), BF16),
            pltpu.VMEM((2 * CAP, D), BF16),
            pltpu.VMEM((2 * CAP, FF), BF16),
            pltpu.VMEM((4, 2, CAP, 128), F32),
            pltpu.VMEM((4, 2, CAP, D), BF16),
            pltpu.VMEM((4, 2, 8, CAP), F32),
            pltpu.VMEM((2, 4, CAP, D), BF16),
            pltpu.VMEM((4, CAP, D), BF16),
            pltpu.VMEM((CAP, D), BF16),
            pltpu.VMEM((5, NX * QUAD, D), BF16),
            pltpu.VMEM((5, NX * QUAD, D), BF16),
            pltpu.VMEM((NZ * TOK, D), F32),
            pltpu.VMEM((2, 8, TOK, D), BF16),
            pltpu.VMEM((2, 8, TOK, D), BF16),
            pltpu.SemaphoreType.DMA((2,)),
            pltpu.SemaphoreType.DMA((COPIES,)),
            pltpu.SemaphoreType.DMA((COPIES,)),
        ],
        compiler_params=pltpu.CompilerParams(
            collective_id=0, has_side_effects=True, vmem_limit_bytes=56 * 1024 * 1024
        ),
        cost_estimate=pl.CostEstimate(
            flops=15_000_000_000, bytes_accessed=5_000_000, transcendentals=0
        ),
    )(tokens, expert_ids.T, gates.T, w_in, w_out)


def solution(mesh):
    tok = P(("grp", "dev"), None)
    return jax.shard_map(
        per_device,
        mesh=mesh,
        in_specs=(tok, tok, tok, P(("grp", "dev"), None, None), P(("grp", "dev"), None, None)),
        out_specs=tok,
        check_vma=False,
    )
```

```python
import jax
import jax.numpy as jnp
from jax import lax
from jax.experimental import pallas as pl
from jax.experimental.pallas import tpu as pltpu
from jax.sharding import PartitionSpec as P

F32 = jnp.float32
BF16 = jnp.bfloat16
NX = 4
NY = 4
NZ = 16
TOK = 64
D = 768
FF = 1536
HIDE = 512
CAP = 256
WIDE = 896
SLOT = 12
QUAD = 48
COPIES = 240
PIECES = 4
PIECE = 16
BATCHES = ((0, 4, 48), (4, 4, 48), (8, 4, 48), (12, 3, 48), (15, 1, 16))
BULK = 768
SLOTS = 832
ORDER = (0, 1, -1, 2, -2, 3, -3, 4, -4, 5, -5, 6, -6, 7, -7, 8)
MESH = pl.DeviceIdType.MESH
NT = (((1,), (1,)), ((), ()))


def iota(shape, dim):
    return lax.broadcasted_iota(jnp.int32, shape, dim)


def ones_where(cond):
    return jnp.where(cond, 1.0, 0.0).astype(BF16)


def mm(a, b):
    return jnp.dot(a, b, preferred_element_type=F32)


def kernel(
    tok_ref,
    ids_ref,
    gates_ref,
    w1_hbm,
    w2_hbm,
    out_ref,
    w1,
    w2,
    column,
    slot_rows,
    select_t,
    stage,
    slots,
    earlier,
    unpack,
    fin,
    lhs,
    hid,
    gain,
    rows,
    row_facts,
    outs,
    peer,
    sums,
    spread,
    back,
    partial_sum,
    ring_in,
    ring_out,
    load_sem,
    send_sem,
    recv_sem,
):
    grp, dev = lax.axis_index("grp"), lax.axis_index("dev")
    x, z = grp // NZ, lax.rem(grp, NZ)
    y, c = dev // 2, lax.rem(dev, 2)
    z_next = (x * NZ + lax.rem(z + 1, NZ), dev)
    z_prev = (x * NZ + lax.rem(z + NZ - 1, NZ), dev)
    x_next = (lax.rem(x + 1, NX) * NZ + z, dev)
    x_prev = (lax.rem(x + NX - 1, NX) * NZ + z, dev)
    y_next = (grp, lax.rem(y + 1, NY) * 2 + c)
    y_prev = (grp, lax.rem(y + NY - 1, NY) * 2 + c)
    twin = (grp, y * 2 + 1 - c)
    y_far = (grp, lax.rem(y + 2, NY) * 2 + c)
    x_far = (lax.rem(x + 2, NX) * NZ + z, dev)

    load1 = pltpu.make_async_copy(w1_hbm.at[0], w1, load_sem.at[0])
    load2 = pltpu.make_async_copy(w2_hbm.at[0], w2, load_sem.at[1])
    load1.start()
    load2.start()

    barrier = pltpu.get_barrier_semaphore()
    for neighbour in (z_next, z_prev, x_next, x_prev, x_far, y_next, y_prev, y_far, twin):
        pl.semaphore_signal(barrier, inc=1, device_id=neighbour, device_id_type=MESH)

    square_r, square_c = iota((TOK, TOK), 0), iota((TOK, TOK), 1)

    def turned(picks):
        return lax.dot_general(
            ones_where(square_r == square_c), picks, NT, preferred_element_type=F32
        ).astype(BF16)

    ids = ids_ref[...]
    to_r, to_c = iota((8, 128), 0), iota((8, 128), 1)
    column[0:TOK, 0:D] = tok_ref[...]
    column[0:TOK, D:WIDE] = (
        mm(
            turned((lax.shift_right_logical(ids, 3) + 1).astype(F32).astype(BF16)),
            ones_where((to_r == 2 * to_c) & (to_c < 4)),
        )
        + mm(
            turned(jnp.bitwise_and(ids, 7).astype(F32).astype(BF16)),
            ones_where(
                ((to_r == 2 * (to_c - 4)) & (to_c < 8)) | ((to_r == 2 * (to_c - 8) + 1) & (to_c < 12))
            ),
        )
        + mm(
            turned(gates_ref[...]),
            ones_where(
                ((to_r == 2 * (to_c - 12)) & (to_c < 16)) | ((to_r == 2 * (to_c - 16) + 1) & (to_c < 20))
            ),
        )
    ).astype(BF16)
    pl.semaphore_wait(barrier, 9)

    started = []
    numbers = iter(range(COPIES))

    def send(src, dst, to):
        k = next(numbers)
        copy = pltpu.make_async_remote_copy(
            src_ref=src,
            dst_ref=dst,
            send_sem=send_sem.at[k],
            recv_sem=recv_sem.at[k],
            device_id=to,
            device_id_type=MESH,
        )
        copy.start()
        started.append(copy)
        return copy

    def block(r, h):
        at = ORDER.index(r if -7 <= r <= 8 else r % NZ)
        return column.at[pl.ds(at * TOK + h * PIECE, PIECE)]

    def pass_on(step, before):
        made = {}
        for h in range(PIECES):
            for way, to in ((1, z_next), (-1, z_prev)):
                if (h, way) in before:
                    before[h, way].wait_recv()
                if step > 8 or step == 8 and (h < PIECES // 2) == (way < 0):
                    continue
                held = -way * (step - 1)
                made[h, way] = send(block(held, h), block(held - way, h), to)
        return made

    tokens_in = pass_on(1, {})
    first_lanes = ones_where(iota((8, 128), 0) == iota((8, 128), 1))
    x_ways = ((2, x_far, 2), (1, x_next, 3), (3, x_prev, 1))

    def eye(n):
        return ones_where(iota((n, n), 0) == iota((n, n), 1))

    def place_batch(q):
        at, owners, part = BATCHES[q]
        n = owners * TOK
        tokens = slice(at * TOK, at * TOK + n)
        group_of = lax.dot_general(
            first_lanes, column[tokens, D:WIDE], NT, preferred_element_type=F32
        )
        hits = jnp.zeros((8, n), F32)
        for i in range(NX):
            target = (lax.rem(x + i, NX) * NZ + z + 1).astype(F32)
            same = jnp.where(group_of == target, 1.0, 0.0)
            hit = same[0:1] + same[1:2] + same[2:3] + same[3:4]
            hits = jnp.where(iota((8, n), 0) == i, hit, hits)
        r, l = iota((n, n), 0), iota((n, n), 1)
        before = ones_where(
            (r < l) & (lax.shift_right_logical(r, 6) == lax.shift_right_logical(l, 6))
        )
        base = (lax.shift_right_logical(iota((8, n), 1), 6) * SLOT).astype(F32)
        slot = jnp.where(hits > 0, mm(hits.astype(BF16), before) + base, -1.0)
        slot_rows[q, :, 0:n] = slot
        slot_id = iota((part, n), 0).astype(F32)
        select = jnp.concatenate(
            [ones_where(slot_id == slot[i : i + 1]) for i in range(NX)], axis=0
        )
        got = mm(select, column[tokens, :]).astype(BF16)
        stage[q, 0 : NX * part, :] = got
        lo = q * NX * QUAD
        slots[lo : lo + part, :] = got[0:part]
        return [
            send(
                stage.at[q, pl.ds(i * part, part)], slots.at[pl.ds(lo + there * part, part)], to
            )
            for i, to, there in x_ways
        ]

    def place_back(q):
        owners, part = BATCHES[q][1:]
        n = owners * TOK
        slot_t = lax.dot_general(
            eye(n), slot_rows[q, :, 0:n].astype(BF16), NT, preferred_element_type=F32
        )
        lane = iota((n, NX * part), 1).astype(F32)
        hot = jnp.zeros((n, NX * part), F32)
        for i in range(NX):
            col = slot_t[:, i : i + 1]
            hot = jnp.where((lane == col + float(i * part)) & (col >= 0), 1.0, hot)
        select_t[q, 0:n, 0 : NX * part] = hot.astype(BF16)

    slots_in = {}
    for step in range(2, 10):
        tokens_in = pass_on(step, tokens_in)
        if step == 2:
            for b in range(BULK // 128):
                shape = (128, BULK)
                earlier[b * 128 : (b + 1) * 128, :] = ones_where(
                    iota(shape, 1) < iota(shape, 0) + b * 128
                )
        if step in (3, 5, 7, 8, 9):
            q = (3, 5, 7, 8, 9).index(step)
            slots_in[q] = place_batch(q)
        if step in (4, 6):
            place_back(step // 2 - 2)
    place_back(2)
    for q in range(4):
        for copy in slots_in[q]:
            copy.wait_recv()

    lane_r, lane_c = iota((128, 128), 0), iota((128, 128), 1)
    repeat = ones_where((jnp.bitwise_and(lane_c, 3) == lane_r) & (lane_c < 20))
    first_four = ones_where(lane_r < 4)
    to_facts = ones_where((lax.shift_right_logical(lane_r, 2) == lane_c + 1) & (lane_r < 20))

    def read_slots(lo, n):
        meta = slots[lo : lo + n, D:WIDE].astype(F32)
        match = ones_where((meta == (grp + 1).astype(F32)) & (iota((n, 128), 1) < 4))
        chosen = (mm(match, repeat) * meta).astype(BF16)
        return mm(match, first_four), mm(chosen, to_facts).astype(BF16)

    def pack_slots(lo, n, place, facts):
        lane_f = iota((n, 128), 1).astype(F32)
        unpack[lo : lo + n, 0:128] = ones_where(place == lane_f)
        unpack[lo : lo + n, 128:256] = ones_where(place == lane_f + 128.0)
        place_t = lax.dot_general(
            ones_where(iota((8, 128), 1) == 0), place.astype(BF16), NT, preferred_element_type=F32
        )
        pack = ones_where(iota((CAP, n), 0).astype(F32) == place_t[0:1])
        return mm(pack, slots[lo : lo + n, 0:D]), mm(pack, facts)

    live, facts = read_slots(0, BULK)
    live_b = live.astype(BF16)
    place = jnp.where(live > 0, mm(earlier[...], live_b), -1.0)
    bulk_rows, bulk_facts = pack_slots(0, BULK, place, facts)
    bulk_count = mm(ones_where(iota((SLOTS - BULK, BULK), 0) >= 0), live_b)
    place_back(3)
    place_back(4)
    for copy in slots_in[4]:
        copy.wait_recv()
    live, facts = read_slots(BULK, SLOTS - BULK)
    shape = (SLOTS - BULK, SLOTS - BULK)
    place = bulk_count + mm(ones_where(iota(shape, 1) < iota(shape, 0)), live.astype(BF16))
    place = jnp.where(live > 0, place, -1.0)
    last_rows, last_facts = pack_slots(BULK, SLOTS - BULK, place, facts)
    rows[0, 0] = (bulk_rows + last_rows).astype(BF16)
    row_facts[0, 0] = lax.dot_general(
        first_lanes, (bulk_facts + last_facts).astype(BF16), NT, preferred_element_type=F32
    )

    def top(r):
        return pl.ds(r * 128, 128)

    f_up = send(row_facts.at[0, 0], row_facts.at[3, 0], y_next)
    f_down = send(row_facts.at[0, 0], row_facts.at[1, 0], y_prev)
    up, down = [], []

    def along_y(r):
        up.append(send(rows.at[0, 0, top(r)], rows.at[3, 0, top(r)], y_next))
        down.append(send(rows.at[0, 0, top(1 - r)], rows.at[1, 0, top(1 - r)], y_prev))

    along_y(0)
    along_y(1)

    def rows_across(i, r):
        return send(rows.at[i, 0, top(r)], rows.at[i, 1, top(r)], twin)

    def facts_across(i):
        return send(row_facts.at[i, 0], row_facts.at[i, 1], twin)

    expert = dev.astype(F32)
    eye_rows = eye(CAP)

    def gains(i):
        for core in range(2):
            f = row_facts[i, core]
            weight = jnp.where(f[0:1] == expert, f[2:3], 0.0) + jnp.where(f[1:2] == expert, f[3:4], 0.0)
            weight = jnp.broadcast_to(weight, (128, CAP)).astype(BF16)
            gain[i, core] = lax.dot_general(eye_rows, weight, NT, preferred_element_type=F32)

    def into_hidden(parts):
        for m, (i, core, r) in enumerate(parts):
            lhs[m * 128 : (m + 1) * 128, :] = rows[i, core, r * 128 : (r + 1) * 128, :]

        def part(n, carry):
            at = pl.ds(pl.multiple_of(n * HIDE, HIDE), HIDE)
            hid[:, at] = jnp.maximum(mm(lhs[...], w1[:, at]), 0.0).astype(BF16)
            return carry

        lax.fori_loop(0, FF // HIDE, part, 0)

    def from_hidden(parts, lo=0):
        def part(n, carry):
            at = pl.ds(pl.multiple_of(n * 256, 256), 256)
            got = mm(hid[lo : lo + len(parts) * 128, :], w2[:, at])
            for m, (i, core, r) in enumerate(parts):
                weight = gain[i, core, r * 128 : (r + 1) * 128, :]
                outs[core, i, r * 128 : (r + 1) * 128, at] = (
                    got[m * 128 : (m + 1) * 128] * jnp.concatenate([weight, weight], axis=1)
                ).astype(BF16)
            return carry

        lax.fori_loop(0, D // 256, part, 0)
        return {
            (i, r): send(outs.at[1, i, top(r)], peer.at[i, top(r)], twin)
            for i, core, r in parts
            if core
        }

    y_ways = {1: (y_next, 3), 2: (y_far, 2), 3: (y_prev, 1)}
    finals = []

    def join_cores(i, r, copy):
        copy.wait_recv()
        rr = slice(r * 128, (r + 1) * 128)
        outs[0, i, rr, :] = (outs[0, i, rr, :].astype(F32) + peer[i, rr, :].astype(F32)).astype(BF16)
        to, there = y_ways[i]
        finals.append(send(outs.at[0, i, top(r)], fin.at[there, top(r)], to))

    def both(*halves):
        return [(i, core, r) for core in (1, 0) for i, r in halves]

    near = both((0, 0), (0, 1))
    early = both((3, 0), (1, 1))
    late = both((3, 1), (1, 0))
    last = both((2, 0), (2, 1))
    waits = [rows_across(0, 0), rows_across(0, 1), facts_across(0)]
    load1.wait()
    load2.wait()
    for copy in waits:
        copy.wait_recv()
    gains(0)
    into_hidden(near)
    near_in = from_hidden(near)
    f_up.wait_recv()
    f_far = send(row_facts.at[3, 0], row_facts.at[2, 0], y_next)
    waits = [facts_across(3)]
    f_down.wait_recv()
    waits.append(facts_across(1))
    for copy in waits:
        copy.wait_recv()
    gains(3)
    gains(1)
    waits = []
    up[0].wait_recv()
    far = [send(rows.at[3, 0, top(0)], rows.at[2, 0, top(0)], y_next)]
    waits.append(rows_across(3, 0))
    down[0].wait_recv()
    far.append(send(rows.at[1, 0, top(1)], rows.at[2, 0, top(1)], y_prev))
    waits.append(rows_across(1, 1))
    for copy in waits:
        copy.wait_recv()
    into_hidden(early)
    early_in = from_hidden(early)
    up[1].wait_recv()
    waits = [rows_across(3, 1)]
    down[1].wait_recv()
    waits.append(rows_across(1, 0))
    f_far.wait_recv()
    waits.append(facts_across(2))
    for copy in waits:
        copy.wait_recv()
    for (i, r), copy in early_in.items():
        join_cores(i, r, copy)
    into_hidden(late)
    gains(2)
    waits = []
    for r in range(2):
        far[r].wait_recv()
        waits.append(rows_across(2, r))
    late_in = from_hidden(late)
    for copy in waits:
        copy.wait_recv()
    for (i, r), copy in late_in.items():
        join_cores(i, r, copy)
    into_hidden(last)
    last_in = from_hidden(last)
    for (i, r), copy in last_in.items():
        join_cores(i, r, copy)
    for copy in near_in.values():
        copy.wait_recv()
    own_sum = outs[0, 0].astype(F32) + peer[0].astype(F32)
    for copy in finals:
        copy.wait_recv()
    sums[...] = (
        own_sum + fin[1].astype(F32) + fin[2].astype(F32) + fin[3].astype(F32)
    ).astype(BF16)

    back_in = {}

    def along_x(q):
        part = BATCHES[q][2]
        lo = q * NX * QUAD
        got = mm(unpack[lo : lo + NX * part, :], sums[...]).astype(BF16)
        spread[q, 0 : NX * part, :] = got
        back[q, 0:part, :] = got[0:part]
        back_in[q] = [
            send(spread.at[q, pl.ds(i * part, part)], back.at[q, pl.ds(there * part, part)], to)
            for i, to, there in x_ways
        ]

    for q in (4, 3, 2, 1, 0):
        along_x(q)
    ready = set()

    def own_part(r, h):
        at = ORDER.index(r)
        q = min(at // 4, 3) if r != 8 else 4
        if q not in ready:
            ready.add(q)
            for copy in back_in[q]:
                copy.wait_recv()
            first, owners, part = BATCHES[q]
            n = owners * TOK
            partial_sum[first * TOK : first * TOK + n, :] = mm(
                select_t[q, 0:n, 0 : NX * part], back[q, 0 : NX * part, :]
            )
        return partial_sum[at * TOK + h * PIECE : at * TOK + (h + 1) * PIECE, :]

    arrived = {}
    for step in range(1, 9):
        current = {}
        for h in range(PIECES):
            part = pl.ds(h * PIECE, PIECE)
            for w, way, to in ((0, -1, z_prev), (1, 1, z_next)):
                if step == 1 and (h < PIECES // 2) != (w == 0):
                    continue
                value = own_part(8 if step == 1 else way * (9 - step), h)
                if (w, h) in arrived:
                    arrived[w, h].wait_recv()
                    value = value + ring_in[w, step - 2, h * PIECE : (h + 1) * PIECE, :].astype(F32)
                ring_out[w, step - 1, h * PIECE : (h + 1) * PIECE, :] = value.astype(BF16)
                current[w, h] = send(ring_out.at[w, step - 1, part], ring_in.at[w, step - 1, part], to)
        arrived = current
    for copy in arrived.values():
        copy.wait_recv()
    out_ref[...] = (
        partial_sum[0:TOK, :] + ring_in[0, 7].astype(F32) + ring_in[1, 7].astype(F32)
    )

    for copy in started:
        copy.wait_send()


def per_device(tokens, expert_ids, gates, w_in, w_out):
    vmem = pl.BlockSpec(memory_space=pltpu.VMEM)
    hbm = pl.BlockSpec(memory_space=pl.ANY)
    return pl.pallas_call(
        kernel,
        out_shape=jax.ShapeDtypeStruct((TOK, D), F32),
        in_specs=[vmem, vmem, vmem, hbm, hbm],
        out_specs=vmem,
        scratch_shapes=[
            pltpu.VMEM((D, FF), BF16),
            pltpu.VMEM((FF, D), BF16),
            pltpu.VMEM((NZ * TOK, WIDE), BF16),
            pltpu.VMEM((5, 8, 256), F32),
            pltpu.VMEM((5, 256, NX * QUAD), BF16),
            pltpu.VMEM((5, NX * QUAD, WIDE), BF16),
            pltpu.VMEM((SLOTS, WIDE), BF16),
            pltpu.VMEM((BULK, BULK), BF16),
            pltpu.VMEM((SLOTS, CAP), BF16),
            pltpu.VMEM((4, CAP, D), BF16),
            pltpu.VMEM((2 * CAP, D), BF16),
            pltpu.VMEM((2 * CAP, FF), BF16),
            pltpu.VMEM((4, 2, CAP, 128), F32),
            pltpu.VMEM((4, 2, CAP, D), BF16),
            pltpu.VMEM((4, 2, 8, CAP), F32),
            pltpu.VMEM((2, 4, CAP, D), BF16),
            pltpu.VMEM((4, CAP, D), BF16),
            pltpu.VMEM((CAP, D), BF16),
            pltpu.VMEM((5, NX * QUAD, D), BF16),
            pltpu.VMEM((5, NX * QUAD, D), BF16),
            pltpu.VMEM((NZ * TOK, D), F32),
            pltpu.VMEM((2, 8, TOK, D), BF16),
            pltpu.VMEM((2, 8, TOK, D), BF16),
            pltpu.SemaphoreType.DMA((2,)),
            pltpu.SemaphoreType.DMA((COPIES,)),
            pltpu.SemaphoreType.DMA((COPIES,)),
        ],
        compiler_params=pltpu.CompilerParams(
            collective_id=0, has_side_effects=True, vmem_limit_bytes=56 * 1024 * 1024
        ),
        cost_estimate=pl.CostEstimate(
            flops=15_000_000_000, bytes_accessed=5_000_000, transcendentals=0
        ),
    )(tokens, expert_ids.T, gates.T, w_in, w_out).astype(BF16)


def solution(mesh):
    tok = P(("grp", "dev"), None)
    return jax.shard_map(
        per_device,
        mesh=mesh,
        in_specs=(tok, tok, tok, P(("grp", "dev"), None, None), P(("grp", "dev"), None, None)),
        out_specs=tok,
        check_vma=False,
    )
```

```python
import jax
import jax.numpy as jnp
from jax import lax
from jax.experimental import pallas as pl
from jax.experimental.pallas import tpu as pltpu
from jax.sharding import PartitionSpec as P

F32 = jnp.float32
BF16 = jnp.bfloat16
NX = 4
NY = 4
NZ = 16
TOK = 64
D = 768
FF = 1536
HIDE = 512
CAP = 256
WIDE = 896
SLOT = 12
QUAD = 48
COPIES = 240
PIECES = 4
PIECE = 16
BATCHES = ((0, 4, 48), (4, 4, 48), (8, 4, 48), (12, 3, 48), (15, 1, 16))
BULK = 768
SLOTS = 832
ORDER = (0, 1, -1, 2, -2, 3, -3, 4, -4, 5, -5, 6, -6, 7, -7, 8)
MESH = pl.DeviceIdType.MESH
NT = (((1,), (1,)), ((), ()))


def iota(shape, dim):
    return lax.broadcasted_iota(jnp.int32, shape, dim)


def ones_where(cond):
    return jnp.where(cond, 1.0, 0.0).astype(BF16)


def mm(a, b):
    return jnp.dot(a, b, preferred_element_type=F32)


def kernel(
    tok_ref,
    ids_ref,
    gates_ref,
    w1_hbm,
    w2_hbm,
    out_ref,
    w1,
    w2,
    column,
    slot_rows,
    select_t,
    stage,
    slots,
    earlier,
    unpack,
    fin,
    lhs,
    hid,
    gain,
    rows,
    row_facts,
    outs,
    peer,
    sums,
    spread,
    back,
    partial_sum,
    ring_in,
    ring_out,
    load_sem,
    send_sem,
    recv_sem,
):
    grp, dev = lax.axis_index("grp"), lax.axis_index("dev")
    x, z = grp // NZ, lax.rem(grp, NZ)
    y, c = dev // 2, lax.rem(dev, 2)
    z_next = (x * NZ + lax.rem(z + 1, NZ), dev)
    z_prev = (x * NZ + lax.rem(z + NZ - 1, NZ), dev)
    x_next = (lax.rem(x + 1, NX) * NZ + z, dev)
    x_prev = (lax.rem(x + NX - 1, NX) * NZ + z, dev)
    y_next = (grp, lax.rem(y + 1, NY) * 2 + c)
    y_prev = (grp, lax.rem(y + NY - 1, NY) * 2 + c)
    twin = (grp, y * 2 + 1 - c)
    y_far = (grp, lax.rem(y + 2, NY) * 2 + c)
    x_far = (lax.rem(x + 2, NX) * NZ + z, dev)

    load1 = pltpu.make_async_copy(w1_hbm.at[0], w1, load_sem.at[0])
    load2 = pltpu.make_async_copy(w2_hbm.at[0], w2, load_sem.at[1])
    load1.start()
    load2.start()

    barrier = pltpu.get_barrier_semaphore()
    for neighbour in (z_next, z_prev, x_next, x_prev, x_far, y_next, y_prev, y_far, twin):
        pl.semaphore_signal(barrier, inc=1, device_id=neighbour, device_id_type=MESH)

    square_r, square_c = iota((TOK, TOK), 0), iota((TOK, TOK), 1)

    def turned(picks):
        return lax.dot_general(
            ones_where(square_r == square_c), picks, NT, preferred_element_type=F32
        ).astype(BF16)

    ids = ids_ref[...]
    to_r, to_c = iota((8, 128), 0), iota((8, 128), 1)
    column[0:TOK, 0:D] = tok_ref[...]
    column[0:TOK, D:WIDE] = (
        mm(
            turned((lax.shift_right_logical(ids, 3) + 1).astype(F32).astype(BF16)),
            ones_where((to_r == 2 * to_c) & (to_c < 4)),
        )
        + mm(
            turned(jnp.bitwise_and(ids, 7).astype(F32).astype(BF16)),
            ones_where(
                ((to_r == 2 * (to_c - 4)) & (to_c < 8)) | ((to_r == 2 * (to_c - 8) + 1) & (to_c < 12))
            ),
        )
        + mm(
            turned(gates_ref[...]),
            ones_where(
                ((to_r == 2 * (to_c - 12)) & (to_c < 16)) | ((to_r == 2 * (to_c - 16) + 1) & (to_c < 20))
            ),
        )
    ).astype(BF16)
    pl.semaphore_wait(barrier, 9)

    started = []
    numbers = iter(range(COPIES))

    def send(src, dst, to):
        k = next(numbers)
        copy = pltpu.make_async_remote_copy(
            src_ref=src,
            dst_ref=dst,
            send_sem=send_sem.at[k],
            recv_sem=recv_sem.at[k],
            device_id=to,
            device_id_type=MESH,
        )
        copy.start()
        started.append(copy)
        return copy

    def block(r, h):
        at = ORDER.index(r if -7 <= r <= 8 else r % NZ)
        return column.at[pl.ds(at * TOK + h * PIECE, PIECE)]

    def pass_on(step, before):
        made = {}
        for h in range(PIECES):
            for way, to in ((1, z_next), (-1, z_prev)):
                if (h, way) in before:
                    before[h, way].wait_recv()
                if step > 8 or step == 8 and (h < PIECES // 2) == (way < 0):
                    continue
                held = -way * (step - 1)
                made[h, way] = send(block(held, h), block(held - way, h), to)
        return made

    tokens_in = pass_on(1, {})
    first_lanes = ones_where(iota((8, 128), 0) == iota((8, 128), 1))
    x_ways = ((2, x_far, 2), (1, x_next, 3), (3, x_prev, 1))

    def eye(n):
        return ones_where(iota((n, n), 0) == iota((n, n), 1))

    def place_batch(q):
        at, owners, part = BATCHES[q]
        n = owners * TOK
        tokens = slice(at * TOK, at * TOK + n)
        group_of = lax.dot_general(
            first_lanes, column[tokens, D:WIDE], NT, preferred_element_type=F32
        )
        hits = jnp.zeros((8, n), F32)
        for i in range(NX):
            target = (lax.rem(x + i, NX) * NZ + z + 1).astype(F32)
            same = jnp.where(group_of == target, 1.0, 0.0)
            hit = same[0:1] + same[1:2] + same[2:3] + same[3:4]
            hits = jnp.where(iota((8, n), 0) == i, hit, hits)
        r, l = iota((n, n), 0), iota((n, n), 1)
        before = ones_where(
            (r < l) & (lax.shift_right_logical(r, 6) == lax.shift_right_logical(l, 6))
        )
        base = (lax.shift_right_logical(iota((8, n), 1), 6) * SLOT).astype(F32)
        slot = jnp.where(hits > 0, mm(hits.astype(BF16), before) + base, -1.0)
        slot_rows[q, :, 0:n] = slot
        slot_id = iota((part, n), 0).astype(F32)
        select = jnp.concatenate(
            [ones_where(slot_id == slot[i : i + 1]) for i in range(NX)], axis=0
        )
        got = mm(select, column[tokens, :]).astype(BF16)
        stage[q, 0 : NX * part, :] = got
        lo = q * NX * QUAD
        slots[lo : lo + part, :] = got[0:part]
        return [
            send(
                stage.at[q, pl.ds(i * part, part)], slots.at[pl.ds(lo + there * part, part)], to
            )
            for i, to, there in x_ways
        ]

    def place_back(q):
        owners, part = BATCHES[q][1:]
        n = owners * TOK
        slot_t = lax.dot_general(
            eye(n), slot_rows[q, :, 0:n].astype(BF16), NT, preferred_element_type=F32
        )
        lane = iota((n, NX * part), 1).astype(F32)
        hot = jnp.zeros((n, NX * part), F32)
        for i in range(NX):
            col = slot_t[:, i : i + 1]
            hot = jnp.where((lane == col + float(i * part)) & (col >= 0), 1.0, hot)
        select_t[q, 0:n, 0 : NX * part] = hot.astype(BF16)

    slots_in = {}
    for step in range(2, 10):
        tokens_in = pass_on(step, tokens_in)
        if step == 2:
            for b in range(BULK // 128):
                shape = (128, BULK)
                earlier[b * 128 : (b + 1) * 128, :] = ones_where(
                    iota(shape, 1) < iota(shape, 0) + b * 128
                )
        if step in (3, 5, 7, 8, 9):
            q = (3, 5, 7, 8, 9).index(step)
            slots_in[q] = place_batch(q)
    for q in range(4):
        for copy in slots_in[q]:
            copy.wait_recv()

    lane_r, lane_c = iota((128, 128), 0), iota((128, 128), 1)
    repeat = ones_where((jnp.bitwise_and(lane_c, 3) == lane_r) & (lane_c < 20))
    first_four = ones_where(lane_r < 4)
    to_facts = ones_where((lax.shift_right_logical(lane_r, 2) == lane_c + 1) & (lane_r < 20))

    def read_slots(lo, n):
        meta = slots[lo : lo + n, D:WIDE].astype(F32)
        match = ones_where((meta == (grp + 1).astype(F32)) & (iota((n, 128), 1) < 4))
        chosen = (mm(match, repeat) * meta).astype(BF16)
        return mm(match, first_four), mm(chosen, to_facts).astype(BF16)

    def pack_slots(lo, n, place, facts):
        lane_f = iota((n, 128), 1).astype(F32)
        unpack[lo : lo + n, 0:128] = ones_where(place == lane_f)
        unpack[lo : lo + n, 128:256] = ones_where(place == lane_f + 128.0)
        place_t = lax.dot_general(
            ones_where(iota((8, 128), 1) == 0), place.astype(BF16), NT, preferred_element_type=F32
        )
        pack = ones_where(iota((CAP, n), 0).astype(F32) == place_t[0:1])
        return mm(pack, slots[lo : lo + n, 0:D]), mm(pack, facts)

    live, facts = read_slots(0, BULK)
    live_b = live.astype(BF16)
    place = jnp.where(live > 0, mm(earlier[...], live_b), -1.0)
    bulk_rows, bulk_facts = pack_slots(0, BULK, place, facts)
    bulk_count = mm(ones_where(iota((SLOTS - BULK, BULK), 0) >= 0), live_b)
    for copy in slots_in[4]:
        copy.wait_recv()
    live, facts = read_slots(BULK, SLOTS - BULK)
    shape = (SLOTS - BULK, SLOTS - BULK)
    place = bulk_count + mm(ones_where(iota(shape, 1) < iota(shape, 0)), live.astype(BF16))
    place = jnp.where(live > 0, place, -1.0)
    last_rows, last_facts = pack_slots(BULK, SLOTS - BULK, place, facts)
    rows[0, 0] = (bulk_rows + last_rows).astype(BF16)
    row_facts[0, 0] = lax.dot_general(
        first_lanes, (bulk_facts + last_facts).astype(BF16), NT, preferred_element_type=F32
    )

    def top(r):
        return pl.ds(r * 128, 128)

    f_up = send(row_facts.at[0, 0], row_facts.at[3, 0], y_next)
    f_down = send(row_facts.at[0, 0], row_facts.at[1, 0], y_prev)
    up, down = [], []

    def along_y(r):
        up.append(send(rows.at[0, 0, top(r)], rows.at[3, 0, top(r)], y_next))
        down.append(send(rows.at[0, 0, top(1 - r)], rows.at[1, 0, top(1 - r)], y_prev))

    along_y(0)
    along_y(1)

    def rows_across(i, r):
        return send(rows.at[i, 0, top(r)], rows.at[i, 1, top(r)], twin)

    def facts_across(i):
        return send(row_facts.at[i, 0], row_facts.at[i, 1], twin)

    expert = dev.astype(F32)
    eye_rows = eye(CAP)

    def gains(i):
        for core in range(2):
            f = row_facts[i, core]
            weight = jnp.where(f[0:1] == expert, f[2:3], 0.0) + jnp.where(f[1:2] == expert, f[3:4], 0.0)
            weight = jnp.broadcast_to(weight, (128, CAP)).astype(BF16)
            gain[i, core] = lax.dot_general(eye_rows, weight, NT, preferred_element_type=F32)

    def into_hidden(parts):
        for m, (i, core, r) in enumerate(parts):
            lhs[m * 128 : (m + 1) * 128, :] = rows[i, core, r * 128 : (r + 1) * 128, :]

        def part(n, carry):
            at = pl.ds(pl.multiple_of(n * HIDE, HIDE), HIDE)
            hid[:, at] = jnp.maximum(mm(lhs[...], w1[:, at]), 0.0).astype(BF16)
            return carry

        lax.fori_loop(0, FF // HIDE, part, 0)

    def from_hidden(parts, lo=0):
        def part(n, carry):
            at = pl.ds(pl.multiple_of(n * 256, 256), 256)
            got = mm(hid[lo : lo + len(parts) * 128, :], w2[:, at])
            for m, (i, core, r) in enumerate(parts):
                weight = gain[i, core, r * 128 : (r + 1) * 128, :]
                outs[core, i, r * 128 : (r + 1) * 128, at] = (
                    got[m * 128 : (m + 1) * 128] * jnp.concatenate([weight, weight], axis=1)
                ).astype(BF16)
            return carry

        lax.fori_loop(0, D // 256, part, 0)
        return {
            (i, r): send(outs.at[1, i, top(r)], peer.at[i, top(r)], twin)
            for i, core, r in parts
            if core
        }

    y_ways = {1: (y_next, 3), 2: (y_far, 2), 3: (y_prev, 1)}
    finals = []

    def join_cores(i, r, copy):
        copy.wait_recv()
        rr = slice(r * 128, (r + 1) * 128)
        outs[0, i, rr, :] = (outs[0, i, rr, :].astype(F32) + peer[i, rr, :].astype(F32)).astype(BF16)
        to, there = y_ways[i]
        finals.append(send(outs.at[0, i, top(r)], fin.at[there, top(r)], to))

    def both(*halves):
        return [(i, core, r) for core in (1, 0) for i, r in halves]

    near = both((0, 0), (0, 1))
    early = both((3, 0), (1, 1))
    late = both((3, 1), (1, 0))
    last = both((2, 0), (2, 1))
    waits = [rows_across(0, 0), rows_across(0, 1), facts_across(0)]
    load1.wait()
    load2.wait()
    for copy in waits:
        copy.wait_recv()
    gains(0)
    into_hidden(near)
    near_in = from_hidden(near)
    f_up.wait_recv()
    f_far = send(row_facts.at[3, 0], row_facts.at[2, 0], y_next)
    waits = [facts_across(3)]
    f_down.wait_recv()
    waits.append(facts_across(1))
    for copy in waits:
        copy.wait_recv()
    gains(3)
    gains(1)
    for q in range(len(BATCHES)):
        place_back(q)
    waits = []
    up[0].wait_recv()
    far = [send(rows.at[3, 0, top(0)], rows.at[2, 0, top(0)], y_next)]
    waits.append(rows_across(3, 0))
    down[0].wait_recv()
    far.append(send(rows.at[1, 0, top(1)], rows.at[2, 0, top(1)], y_prev))
    waits.append(rows_across(1, 1))
    for copy in waits:
        copy.wait_recv()
    into_hidden(early)
    early_in = from_hidden(early)
    up[1].wait_recv()
    waits = [rows_across(3, 1)]
    down[1].wait_recv()
    waits.append(rows_across(1, 0))
    f_far.wait_recv()
    waits.append(facts_across(2))
    for copy in waits:
        copy.wait_recv()
    for (i, r), copy in early_in.items():
        join_cores(i, r, copy)
    into_hidden(late)
    gains(2)
    waits = []
    for r in range(2):
        far[r].wait_recv()
        waits.append(rows_across(2, r))
    late_in = from_hidden(late)
    for copy in waits:
        copy.wait_recv()
    for (i, r), copy in late_in.items():
        join_cores(i, r, copy)
    into_hidden(last)
    last_in = from_hidden(last)
    for (i, r), copy in last_in.items():
        join_cores(i, r, copy)
    for copy in near_in.values():
        copy.wait_recv()
    own_sum = outs[0, 0].astype(F32) + peer[0].astype(F32)
    for copy in finals:
        copy.wait_recv()
    sums[...] = (
        own_sum + fin[1].astype(F32) + fin[2].astype(F32) + fin[3].astype(F32)
    ).astype(BF16)

    back_in = {}

    def along_x(q):
        part = BATCHES[q][2]
        lo = q * NX * QUAD
        got = mm(unpack[lo : lo + NX * part, :], sums[...]).astype(BF16)
        spread[q, 0 : NX * part, :] = got
        back[q, 0:part, :] = got[0:part]
        back_in[q] = [
            send(spread.at[q, pl.ds(i * part, part)], back.at[q, pl.ds(there * part, part)], to)
            for i, to, there in x_ways
        ]

    for q in (4, 3, 2, 1, 0):
        along_x(q)
    ready = set()

    def own_part(r, h):
        at = ORDER.index(r)
        q = min(at // 4, 3) if r != 8 else 4
        if q not in ready:
            ready.add(q)
            for copy in back_in[q]:
                copy.wait_recv()
            first, owners, part = BATCHES[q]
            n = owners * TOK
            partial_sum[first * TOK : first * TOK + n, :] = mm(
                select_t[q, 0:n, 0 : NX * part], back[q, 0 : NX * part, :]
            )
        return partial_sum[at * TOK + h * PIECE : at * TOK + (h + 1) * PIECE, :]

    arrived = {}
    for step in range(1, 9):
        current = {}
        for h in range(PIECES):
            part = pl.ds(h * PIECE, PIECE)
            for w, way, to in ((0, -1, z_prev), (1, 1, z_next)):
                if step == 1 and (h < PIECES // 2) != (w == 0):
                    continue
                value = own_part(8 if step == 1 else way * (9 - step), h)
                if (w, h) in arrived:
                    arrived[w, h].wait_recv()
                    value = value + ring_in[w, step - 2, h * PIECE : (h + 1) * PIECE, :].astype(F32)
                ring_out[w, step - 1, h * PIECE : (h + 1) * PIECE, :] = value.astype(BF16)
                current[w, h] = send(ring_out.at[w, step - 1, part], ring_in.at[w, step - 1, part], to)
        arrived = current
    for copy in arrived.values():
        copy.wait_recv()
    out_ref[...] = (
        partial_sum[0:TOK, :] + ring_in[0, 7].astype(F32) + ring_in[1, 7].astype(F32)
    )

    for copy in started:
        copy.wait_send()


def per_device(tokens, expert_ids, gates, w_in, w_out):
    vmem = pl.BlockSpec(memory_space=pltpu.VMEM)
    hbm = pl.BlockSpec(memory_space=pl.ANY)
    return pl.pallas_call(
        kernel,
        out_shape=jax.ShapeDtypeStruct((TOK, D), F32),
        in_specs=[vmem, vmem, vmem, hbm, hbm],
        out_specs=vmem,
        scratch_shapes=[
            pltpu.VMEM((D, FF), BF16),
            pltpu.VMEM((FF, D), BF16),
            pltpu.VMEM((NZ * TOK, WIDE), BF16),
            pltpu.VMEM((5, 8, 256), F32),
            pltpu.VMEM((5, 256, NX * QUAD), BF16),
            pltpu.VMEM((5, NX * QUAD, WIDE), BF16),
            pltpu.VMEM((SLOTS, WIDE), BF16),
            pltpu.VMEM((BULK, BULK), BF16),
            pltpu.VMEM((SLOTS, CAP), BF16),
            pltpu.VMEM((4, CAP, D), BF16),
            pltpu.VMEM((2 * CAP, D), BF16),
            pltpu.VMEM((2 * CAP, FF), BF16),
            pltpu.VMEM((4, 2, CAP, 128), F32),
            pltpu.VMEM((4, 2, CAP, D), BF16),
            pltpu.VMEM((4, 2, 8, CAP), F32),
            pltpu.VMEM((2, 4, CAP, D), BF16),
            pltpu.VMEM((4, CAP, D), BF16),
            pltpu.VMEM((CAP, D), BF16),
            pltpu.VMEM((5, NX * QUAD, D), BF16),
            pltpu.VMEM((5, NX * QUAD, D), BF16),
            pltpu.VMEM((NZ * TOK, D), F32),
            pltpu.VMEM((2, 8, TOK, D), BF16),
            pltpu.VMEM((2, 8, TOK, D), BF16),
            pltpu.SemaphoreType.DMA((2,)),
            pltpu.SemaphoreType.DMA((COPIES,)),
            pltpu.SemaphoreType.DMA((COPIES,)),
        ],
        compiler_params=pltpu.CompilerParams(
            collective_id=0, has_side_effects=True, vmem_limit_bytes=56 * 1024 * 1024
        ),
        cost_estimate=pl.CostEstimate(
            flops=15_000_000_000, bytes_accessed=5_000_000, transcendentals=0
        ),
    )(tokens, expert_ids.T, gates.T, w_in, w_out).astype(BF16)


def solution(mesh):
    tok = P(("grp", "dev"), None)
    return jax.shard_map(
        per_device,
        mesh=mesh,
        in_specs=(tok, tok, tok, P(("grp", "dev"), None, None), P(("grp", "dev"), None, None)),
        out_specs=tok,
        check_vma=False,
    )
```
